32 devices in a mesh: seg: 8 (over y, x, core), blk: 4 (over z).
Axes of the slice: x: 2, y: 2, z: 4, core: 2. Of those that a mesh axis runs over, the one named last changes fastest.
Arguments:
- two_site: float32 [8, 4, 128, 128], P('seg', 'blk'), may hold values from -6 to 6
- diag_left: float32 [8, 4, 2, 128, 128], P('seg', 'blk')
- diag_right: float32 [8, 4, 2, 128, 128], P('seg', 'blk')
- hop_left: float32 [8, 4, 16, 128, 128], P('seg', 'blk'), may hold values from -0.125 to 0.125
- hop_right: float32 [8, 4, 16, 128, 128], P('seg', 'blk'), may hold values from -0.125 to 0.125
- sector_sizes: int32 [8, 4], P('seg', 'blk'), may hold values from 1 to 128, 384 in all within a row
- ranks: int32 [8, 4], P('seg', 'blk'), may hold values from 1 to 128
Outputs:
- new_state: float32 [8, 4, 128, 128], P('seg', 'blk')
- left_boundary: float32 [8, 4, 18, 128, 128], P('seg', 'blk')
- right_boundary: float32 [8, 4, 18, 128, 128], P('seg', 'blk')
- energy: float32 [8], P('seg')
The draws below stay inside these ranges and needn't reach their ends.
Inputs may be any that keep to these rules, and one draw needn't show every extreme that they name: Each row of sector_sizes sums to 384; the largest entry of every row is 128.
All inputs are finite; a program needn't handle non-finite values. No bound on the sum of `sector_sizes` on one device may be relied on, other than what follows from the above.
Results may differ from the reference program's by a relative error of at most 0.0003.
Values sent between devices are 32-bit elements; how exact they have to be, the bound alone decides.
A program may use at most 64 MiB of HBM per device.

```python
import math
import jax
import jax.numpy as jnp
import numpy as np
from jax import lax

P_SIZE = 128
DIAG = 2
HOP = 16
ITERS = 4
NSEG = 8
NSEC = 4
CHI = 384


def symmetric_part(random_part):
    return (random_part + jnp.swapaxes(random_part, -1, -2)) / math.sqrt(2.0 * P_SIZE)


def draw_diag_left(key, part):
    key = jax.random.fold_in(key, 5)
    full_shape = (NSEG, NSEC, DIAG, P_SIZE, P_SIZE)
    random_part = jax.random.normal(key, full_shape, jnp.float32)
    return symmetric_part(random_part)


def draw_diag_right(key, part):
    key = jax.random.fold_in(key, 9)
    full_shape = (NSEG, NSEC, DIAG, P_SIZE, P_SIZE)
    random_part = jax.random.normal(key, full_shape, jnp.float32)
    return symmetric_part(random_part)


def with_ends(array, own_key, least, top_value):
    spot = [jax.random.randint(jax.random.fold_in(own_key, axis), (), 0, length) for axis, length in enumerate(array.shape)]
    longest = array.shape.index(max(array.shape))
    neighbour = spot[:longest] + [(spot[longest] + 1) % array.shape[longest]] + spot[longest + 1:]
    return array.at[tuple(spot)].set(least).at[tuple(neighbour)].set(top_value)


def block_scale(stream_key, dims, shards, smallest, top_value):
    factor_of = 1.0
    for position, blocks in shards:
        steps = jax.random.uniform(jax.random.fold_in(jax.random.fold_in(stream_key, 6), position), (blocks,), jnp.float32, smallest / len(shards), top_value / len(shards))
        factor_of = factor_of * jnp.repeat(jnp.exp(steps), dims[position] // blocks).reshape((-1,) + (1,) * (len(dims) - 1 - position))
    return factor_of


def split_up(amount, total, most, skew):
    portions = [(1 << 20) // math.isqrt(standing ** skew) + 1 for standing in range(2, amount + 1)]
    spare, given = total - most - (amount - 1), [1] * (amount - 1)
    while spare > 0:
        candidates = [i for i in range(amount - 1) if given[i] < most]
        whole, budget = sum([portions[i] for i in candidates]), spare
        for i in candidates:
            addition = min(most - given[i], max(1, budget * portions[i] // whole), spare)
            given[i] = given[i] + addition
            spare = spare - addition
    return np.array([most] + given)


def ragged_sizes(stream_key, amount, total, most, slope):
    if amount == 2:
        one = jax.random.randint(stream_key, (), max(1, total - most), min(most, total - 1) + 1)
        return jnp.stack([one, total - one])
    lengths = jnp.asarray(split_up(amount, total, most, slope), jnp.int32)
    twos = (amount - 1) // 2
    giver, receiver = lengths[1:1 + 2 * twos:2], lengths[2:2 + 2 * twos:2]
    margin = jnp.minimum(giver - 1, most - receiver)
    moved = jax.random.randint(jax.random.fold_in(stream_key, 1), (twos,), 0, 1 << 20) % (margin + 1)
    lengths = lengths.at[1:1 + 2 * twos:2].set(giver - moved).at[2:2 + 2 * twos:2].set(receiver + moved)
    return lengths[jax.random.permutation(jax.random.fold_in(stream_key, 2), amount)]


def scatter_about(key, dims, width, limit, split=(), held_as=jnp.bfloat16):
    result = jax.random.normal(key, dims, jnp.float32) * width
    if len(split) > 0:
        result = block_scale(key, dims, split, -0.22, 0.18) * result
    return jnp.clip(result, min=-limit, max=limit).astype(held_as)


def setup_inputs(seed: int = 0) -> dict:
    streams_of = jax.random.split(jax.random.key(seed), 8)
    two_site = scatter_about(streams_of[0], (NSEG, NSEC, P_SIZE, P_SIZE), 1.0, 6.0, ((0, 8), (1, 4)), jnp.float32)
    diag_left = draw_diag_left(jax.random.fold_in(streams_of[7], 71), 0)
    diag_right = draw_diag_right(jax.random.fold_in(streams_of[7], 71), 0)
    hop_left = scatter_about(streams_of[3], (NSEG, NSEC, HOP, P_SIZE, P_SIZE), (HOP * P_SIZE) ** -0.5, 0.125, ((0, 8), (1, 4)), jnp.float32)
    hop_right = scatter_about(streams_of[4], (NSEG, NSEC, HOP, P_SIZE, P_SIZE), (HOP * P_SIZE) ** -0.5, 0.125, ((0, 8), (1, 4)), jnp.float32)
    sector_sizes = jax.vmap(lambda own: ragged_sizes(own, NSEC, CHI, P_SIZE, 1))(jax.random.split(streams_of[5], NSEG)).reshape((NSEG, NSEC)).astype(jnp.int32)
    ranks = with_ends(jax.random.randint(streams_of[6], (NSEG, NSEC), 1, P_SIZE + 1), jax.random.fold_in(streams_of[6], 1), 1, P_SIZE).astype(jnp.int32)
    return {"two_site": two_site, "diag_left": diag_left, "diag_right": diag_right, "hop_left": hop_left, "hop_right": hop_right, "sector_sizes": sector_sizes, "ranks": ranks}


highest = lax.Precision.HIGHEST
spectral_shift = 20.0

def channel_apply(left_ops, vector, right_ops):
    halfway = jnp.einsum('qwij,qjk->qwik', left_ops, vector, precision=highest)
    return jnp.einsum('qwik,qwlk->qil', halfway, right_ops, precision=highest)

def channel_adjoint(left_ops, vector, right_ops):
    halfway = jnp.einsum('qwji,qjk->qwik', left_ops, vector, precision=highest)
    return jnp.einsum('qwik,qwkl->qil', halfway, right_ops, precision=highest)

def left_extend(kept_state, left_ops):
    halfway = jnp.einsum('qwij,qjl->qwil', left_ops, kept_state, precision=highest)
    return jnp.einsum('qik,qwil->qwkl', kept_state, halfway, precision=highest)

def right_extend(kept_state, right_ops):
    halfway = jnp.einsum('qik,qwlk->qwil', kept_state, right_ops, precision=highest)
    return jnp.einsum('qwil,qjl->qwij', halfway, kept_state, precision=highest)

def apply_ham(vector, diag_left, diag_right, hop_left, hop_right, live_mask):
    own_terms = channel_apply(diag_left, vector, diag_right)
    nothing = jnp.zeros_like(vector[:1])
    previous = jnp.concatenate([nothing, vector[:-1]], 0)
    carried = channel_adjoint(hop_left, vector, hop_right)
    following = jnp.concatenate([carried[1:], nothing], 0)
    return live_mask * (own_terms + channel_apply(hop_left, previous, hop_right) + following)

def segment_update(pieces):
    two_site, diag_left, diag_right, hop_left, hop_right, sector_size, sector_rank = pieces
    positions = jnp.arange(P_SIZE, dtype=jnp.int32)
    row_live = (positions[None, :] < sector_size[:, None]).astype(jnp.float32)
    live_mask = row_live[:, :, None] * row_live[:, None, :]
    vector = live_mask * two_site
    energy = jnp.zeros((), jnp.float32)
    for iteration in range(ITERS):
        applied = apply_ham(vector, diag_left, diag_right, hop_left, hop_right, live_mask)
        energy = jnp.sum(vector * applied) / jnp.sum(vector * vector)
        vector = spectral_shift * vector - applied
    bond_total = jnp.sum(sector_size).astype(jnp.float32)
    new_state = vector * jnp.sqrt(bond_total * P_SIZE / jnp.sum(vector * vector))
    kept_count = jnp.minimum(sector_rank, sector_size)
    col_live = (positions[None, :] < kept_count[:, None]).astype(jnp.float32)
    kept_state = new_state * col_live[:, None, :]
    scale = 1.0 / jnp.sqrt(jnp.float32(P_SIZE))
    new_left = jnp.concatenate([left_extend(kept_state, diag_left), left_extend(kept_state, hop_left)], 1) * scale
    new_right = jnp.concatenate([right_extend(kept_state, diag_right), right_extend(kept_state, hop_right)], 1) * scale
    return (new_state, new_left, new_right, energy)

def reference(two_site, diag_left, diag_right, hop_left, hop_right, sector_sizes, ranks):
    new_state, new_left, new_right, energy = lax.map(segment_update, (two_site, diag_left, diag_right, hop_left, hop_right, sector_sizes, ranks))
    left_boundary = jnp.concatenate([jnp.zeros_like(new_left[:1]), new_left[:-1]], 0)
    right_boundary = jnp.concatenate([new_right[1:], jnp.zeros_like(new_right[:1])], 0)
    return (new_state, left_boundary, right_boundary, energy)
```

```python
import functools

import jax
import jax.numpy as jnp
from jax import lax
from jax.experimental import pallas as pl
from jax.experimental.pallas import tpu as pltpu
from jax.sharding import PartitionSpec as P

ITERS = 4
MESH = pl.DeviceIdType.MESH
f32 = jnp.float32
bf16 = jnp.bfloat16
spectral_shift = 20.0


def split(x):
    hi = x.astype(bf16)
    lo = (x - hi.astype(f32)).astype(bf16)
    return hi, lo


def stationary(x):
    hi, lo = split(x)
    top = jnp.concatenate([hi, lo], 1)
    low = jnp.concatenate([hi, jnp.zeros_like(hi)], 1)
    return jnp.concatenate([top, low], 0)


def streamed(x):
    hi, lo = split(x)
    top = jnp.concatenate([hi, hi], 1)
    low = jnp.concatenate([lo, jnp.zeros_like(lo)], 1)
    return jnp.concatenate([top, low], 0)


def dot(a, b):
    return jnp.dot(a, b, preferred_element_type=f32)


def prepare(source, rows, target, at, transpose, n):
    x = source[pl.ds(rows, n), :]
    hi, lo = split(x.T if transpose else x)
    target[pl.ds(at, n), 0:n] = hi
    target[pl.ds(at, n), n : 2 * n] = lo


def first_stage(ops, start, count, weight, held, column, n):
    for c in range(0, count, 2):
        got = dot(ops[start + c * n : start + (c + 2) * n, :], weight)
        got = got[:, 0:n] + got[:, n : 2 * n]
        hi, lo = split(got)
        for part in range(2):
            lanes = column + (c + part) * n
            held[0:n, lanes : lanes + n] = hi[part * n : (part + 1) * n]
            held[n : 2 * n, lanes : lanes + n] = lo[part * n : (part + 1) * n]


def second_stage(held, column, count, ops, start, n):
    got = dot(held[:, column : column + count * n], ops[start : start + count * n, :])
    return (got[0:n, 0:n] + got[0:n, n : 2 * n]) + (got[n : 2 * n, 0:n] + got[n : 2 * n, n : 2 * n])


def extend(ops, state, state_t, out, scale, count, n):
    weight = stationary(state)
    rows = streamed(state_t)
    for c in range(0, count, 2):
        got = dot(ops[c * n : (c + 2) * n, :], weight)
        got = got[:, 0:n] + got[:, n : 2 * n]
        hi, lo = split(got)
        pair = jnp.concatenate(
            [jnp.concatenate([hi[0:n], hi[n:]], 1), jnp.concatenate([lo[0:n], lo[n:]], 1)], 0
        )
        done = dot(rows, pair)
        done = (done[0:n] + done[n:]) * scale
        out[c * n : (c + 1) * n, :] = done[:, 0:n]
        out[(c + 1) * n : (c + 2) * n, :] = done[:, n : 2 * n]


def kernel(
    nseg, nblk, ndiag, nhop, n,
    size_ref, rank_ref, two_ref, dl_ref, dr_ref, hl_ref, hr_ref,
    state_ref, lb_ref, rb_ref, energy_ref,
    xl, yr, far_x, far_y, a2, at2, b2, bt2, fx2, fy2, held,
    v_buf, c_buf, rv, rc, kept, far_kept, sums,
    load_sem, v_send, v_recv, c_send, c_recv, x_send, x_recv, k_send, k_recv, s_send, s_recv,
):
    s = lax.axis_index("seg")
    q = lax.axis_index("blk")
    nch = ndiag + nhop
    small = ndiag * n

    loads = [
        pltpu.make_async_copy(src, dst, load_sem.at[i])
        for i, (src, dst) in enumerate(
            (
                (two_ref, c_buf.at[ITERS]),
                (hl_ref, xl.at[pl.ds(small, nhop * n)]),
                (hr_ref, yr.at[pl.ds(small, nhop * n)]),
                (dl_ref, xl.at[pl.ds(0, small)]),
                (dr_ref, yr.at[pl.ds(0, small)]),
            )
        )
    ]
    for load in loads:
        load.start()

    def per_segment(action):
        action(0)
        pl.when(s < nseg - 1)(lambda: action(1))
        pl.when(s > 0)(lambda: action(-1))

    def per_peer(step, action):
        def body(j, carry):
            action(lax.rem(q + j, nblk), j)
            return carry

        lax.fori_loop(1 if step == 0 else 0, nblk, body, 0, unroll=nblk <= 8)

    barrier = pltpu.get_barrier_semaphore()

    def greet(step):
        per_peer(
            step,
            lambda peer, j: pl.semaphore_signal(
                barrier, inc=1, device_id={"seg": s + step, "blk": peer}, device_id_type=MESH
            ),
        )

    per_segment(greet)

    @pl.when(q == 0)
    def _():
        rv[...] = jnp.zeros_like(rv)

    @pl.when(q == nblk - 1)
    def _():
        rc[...] = jnp.zeros_like(rc)

    size = size_ref[0, 0]
    count = jnp.minimum(rank_ref[0, 0], size)
    row_at = lax.broadcasted_iota(jnp.int32, (n, n), 0)
    col_at = lax.broadcasted_iota(jnp.int32, (n, n), 1)
    live = jnp.where(jnp.maximum(row_at, col_at) < size, 1.0, 0.0).astype(f32)
    col_live = jnp.where(col_at < count, 1.0, 0.0).astype(f32)

    loads[0].wait()
    v_buf[0] = live * c_buf[ITERS]

    groups = 1 + jnp.minimum(s, 1) + jnp.minimum(nseg - 1 - s, 1)
    pl.semaphore_wait(barrier, groups * nblk - 1)

    def remote(src, dst, send, recv, where):
        return pltpu.make_async_remote_copy(
            src_ref=src, dst_ref=dst, send_sem=send, recv_sem=recv,
            device_id=where, device_id_type=MESH,
        )

    def send_v(k):
        return remote(v_buf.at[k], rv.at[k], v_send.at[k], v_recv.at[k], {"seg": s, "blk": q + 1})

    def send_c(k):
        return remote(c_buf.at[k], rc.at[k], c_send.at[k], c_recv.at[k], {"seg": s, "blk": q - 1})

    up, down = {"seg": s + 1, "blk": q}, {"seg": s - 1, "blk": q}
    to_up = [
        remote(dl_ref, far_x.at[pl.ds(0, small)], x_send.at[0], x_recv.at[0], up),
        remote(hl_ref, far_x.at[pl.ds(small, nhop * n)], x_send.at[1], x_recv.at[1], up),
    ]
    to_down = [
        remote(dr_ref, far_y.at[pl.ds(0, small)], x_send.at[2], x_recv.at[2], down),
        remote(hr_ref, far_y.at[pl.ds(small, nhop * n)], x_send.at[3], x_recv.at[3], down),
    ]
    kept_up = remote(kept, far_kept.at[0], k_send.at[0], k_recv.at[0], up)
    kept_down = remote(kept, far_kept.at[1], k_send.at[1], k_recv.at[1], down)

    has_next, has_previous = q < nblk - 1, q > 0
    has_up, has_down = s < nseg - 1, s > 0

    pl.when(has_next)(lambda: send_v(0).start())

    @pl.when(has_up)
    def _():
        for copy in to_up:
            copy.start()

    @pl.when(has_down)
    def _():
        for copy in to_down:
            copy.start()

    loads[1].wait()
    loads[2].wait()
    for h in range(nhop):
        at = small + h * n
        prepare(xl, at, at2, h * n, True, n)
        prepare(yr, at, b2, h * n, False, n)

    def carried(k):
        first_stage(at2, 0, nhop, stationary(v_buf[k]), held, 0, n)
        c_buf[k] = second_stage(held, 0, nhop, b2, 0, n)
        pl.when(has_previous)(lambda: send_c(k).start())

    def finish(k):
        first_stage(a2, 0, ndiag, stationary(v_buf[k]), held, 0, n)
        pl.when(has_previous)(lambda: send_v(k).wait_recv())
        first_stage(a2, small, nhop, stationary(rv[k]), held, small, n)
        own = second_stage(held, 0, nch, bt2, 0, n)
        pl.when(has_next)(lambda: send_c(k).wait_recv())
        applied = live * (own + rc[k])
        vector = spectral_shift * v_buf[k] - applied
        v_buf[k + 1] = vector
        return applied, vector

    carried(0)
    loads[3].wait()
    loads[4].wait()
    for c in range(nch):
        prepare(xl, c * n, a2, c * n, False, n)
        prepare(yr, c * n, bt2, c * n, True, n)
    finish(0)
    pl.when(has_next)(lambda: send_v(1).start())

    def middle(k, carry):
        carried(k)
        finish(k)
        pl.when(has_next)(lambda: send_v(k + 1).start())
        return carry

    lax.fori_loop(1, ITERS - 1, middle, 0)
    carried(ITERS - 1)
    applied, vector = finish(ITERS - 1)
    last = v_buf[ITERS - 1]
    kept[...] = vector * col_live
    pl.when(has_up)(lambda: kept_up.start())
    pl.when(has_down)(lambda: kept_down.start())

    def rowsum(x):
        return jnp.sum(x, 0, keepdims=True)

    row8 = lax.broadcasted_iota(jnp.int32, (8, n), 0)
    tile = jnp.where(row8 == 0, rowsum(last * applied), 0.0)
    tile = jnp.where(row8 == 1, rowsum(last * last), tile)
    tile = jnp.where(row8 == 2, rowsum(vector * vector), tile)
    tile = jnp.where(row8 == 3, size.astype(f32) * (1.0 / n), tile)
    sums[1, q] = tile

    def sum_copy(step, peer, j):
        group = 1 - step
        return remote(
            sums.at[1, q], sums.at[group, q], s_send.at[group, j], s_recv.at[group, q],
            {"seg": s + step, "blk": peer},
        )

    def sum_arrival(group, peer):
        return remote(
            sums.at[1, q], sums.at[group, peer], s_send.at[group, 0], s_recv.at[group, peer],
            {"seg": s, "blk": peer},
        )

    per_segment(lambda step: per_peer(step, lambda peer, j: sum_copy(step, peer, j).start()))

    @pl.when(has_down)
    def _():
        for copy in to_up:
            copy.wait_recv()
        for c in range(nch):
            prepare(far_x, c * n, fx2, c * n, False, n)

    @pl.when(has_up)
    def _():
        for copy in to_down:
            copy.wait_recv()
        for c in range(nch):
            prepare(far_y, c * n, fy2, c * n, True, n)

    def totals(group):
        step = 0 if group == 1 else 1
        per_peer(step, lambda peer, j: sum_arrival(group, peer).wait_recv())
        total = sums[group, 0]
        for j in range(1, nblk):
            total = total + sums[group, j]
        return jnp.sum(total, 1, keepdims=True)

    def norm(total):
        return jnp.sqrt(total[3:4] * n / total[2:3])

    own = totals(1)
    state_ref[...] = vector * norm(own)
    energy_ref[...] = own[0:1] / own[1:2]
    scale = 1.0 / jnp.sqrt(f32(n))

    @pl.when(has_down)
    def _():
        kept_up.wait_recv()
        k = far_kept[0] * norm(totals(0))
        extend(fx2, k, k.T, lb_ref, scale, nch, n)

    @pl.when(s == 0)
    def _():
        lb_ref[...] = jnp.zeros_like(lb_ref)

    @pl.when(has_up)
    def _():
        kept_down.wait_recv()
        k = far_kept[1] * norm(totals(2))
        extend(fy2, k.T, k, rb_ref, scale, nch, n)

    @pl.when(s == nseg - 1)
    def _():
        rb_ref[...] = jnp.zeros_like(rb_ref)

    @pl.when(has_next)
    def _():
        for k in range(ITERS):
            send_v(k).wait_send()

    @pl.when(has_previous)
    def _():
        for k in range(ITERS):
            send_c(k).wait_send()

    @pl.when(has_up)
    def _():
        for copy in to_up + [kept_up]:
            copy.wait_send()

    @pl.when(has_down)
    def _():
        for copy in to_down + [kept_down]:
            copy.wait_send()

    per_segment(lambda step: per_peer(step, lambda peer, j: sum_copy(step, peer, j).wait_send()))


def shards(nseg, nblk, two_site, diag_left, diag_right, hop_left, hop_right, sector_sizes, ranks):
    n = two_site.shape[2]
    ndiag, nhop = diag_left.shape[2], hop_left.shape[2]
    nch = ndiag + nhop
    smem = pl.BlockSpec(memory_space=pltpu.SMEM)
    vmem = pl.BlockSpec(memory_space=pltpu.VMEM)
    anywhere = pl.BlockSpec(memory_space=pl.ANY)
    dma = pltpu.SemaphoreType.DMA
    state, left, right, energy = pl.pallas_call(
        functools.partial(kernel, nseg, nblk, ndiag, nhop, n),
        out_shape=(
            jax.ShapeDtypeStruct((n, n), f32),
            jax.ShapeDtypeStruct((nch * n, n), f32),
            jax.ShapeDtypeStruct((nch * n, n), f32),
            jax.ShapeDtypeStruct((1, 1), f32),
        ),
        in_specs=[smem, smem] + [anywhere] * 5,
        out_specs=(vmem, vmem, vmem, vmem),
        scratch_shapes=[
            pltpu.VMEM((nch * n, n), f32),
            pltpu.VMEM((nch * n, n), f32),
            pltpu.VMEM((nch * n, n), f32),
            pltpu.VMEM((nch * n, n), f32),
            pltpu.VMEM((nch * n, 2 * n), bf16),
            pltpu.VMEM((nhop * n, 2 * n), bf16),
            pltpu.VMEM((nhop * n, 2 * n), bf16),
            pltpu.VMEM((nch * n, 2 * n), bf16),
            pltpu.VMEM((nch * n, 2 * n), bf16),
            pltpu.VMEM((nch * n, 2 * n), bf16),
            pltpu.VMEM((2 * n, nch * n), bf16),
            pltpu.VMEM((ITERS + 1, n, n), f32),
            pltpu.VMEM((ITERS + 1, n, n), f32),
            pltpu.VMEM((ITERS, n, n), f32),
            pltpu.VMEM((ITERS, n, n), f32),
            pltpu.VMEM((n, n), f32),
            pltpu.VMEM((2, n, n), f32),
            pltpu.VMEM((3, nblk, 8, n), f32),
            dma((5,)),
            dma((ITERS,)),
            dma((ITERS,)),
            dma((ITERS,)),
            dma((ITERS,)),
            dma((4,)),
            dma((4,)),
            dma((2,)),
            dma((2,)),
            dma((3, nblk)),
            dma((3, nblk)),
        ],
        compiler_params=pltpu.CompilerParams(
            collective_id=0, has_side_effects=True, vmem_limit_bytes=40 * 1024 * 1024
        ),
        name="solve",
    )(
        sector_sizes, ranks,
        two_site.reshape(n, n),
        diag_left.reshape(ndiag * n, n),
        diag_right.reshape(ndiag * n, n),
        hop_left.reshape(nhop * n, n),
        hop_right.reshape(nhop * n, n),
    )
    return (
        state.reshape(1, 1, n, n),
        left.reshape(1, 1, nch, n, n),
        right.reshape(1, 1, nch, n, n),
        energy.reshape(1),
    )


def solution(mesh):
    nseg, nblk = mesh.shape["seg"], mesh.shape["blk"]
    return jax.shard_map(
        functools.partial(shards, nseg, nblk),
        mesh=mesh,
        in_specs=(
            P("seg", "blk", None, None),
            P("seg", "blk", None, None, None),
            P("seg", "blk", None, None, None),
            P("seg", "blk", None, None, None),
            P("seg", "blk", None, None, None),
            P("seg", "blk"),
            P("seg", "blk"),
        ),
        out_specs=(
            P("seg", "blk", None, None),
            P("seg", "blk", None, None, None),
            P("seg", "blk", None, None, None),
            P("seg"),
        ),
        check_vma=False,
    )
```

```python
import functools

import jax
import jax.numpy as jnp
from jax import lax
from jax.experimental import pallas as pl
from jax.experimental.pallas import tpu as pltpu
from jax.sharding import PartitionSpec as P

ITERS = 4
BATCH = 8
MESH = pl.DeviceIdType.MESH
f32 = jnp.float32
bf16 = jnp.bfloat16
spectral_shift = 20.0


def split(x):
    hi = x.astype(bf16)
    lo = (x - hi.astype(f32)).astype(bf16)
    return hi, lo


def stationary(x):
    hi, lo = split(x)
    top = jnp.concatenate([hi, lo], 1)
    low = jnp.concatenate([hi, jnp.zeros_like(hi)], 1)
    return jnp.concatenate([top, low], 0)


def streamed(x):
    hi, lo = split(x)
    top = jnp.concatenate([hi, hi], 1)
    low = jnp.concatenate([lo, jnp.zeros_like(lo)], 1)
    return jnp.concatenate([top, low], 0)


def dot(a, b):
    return jnp.dot(a, b, preferred_element_type=f32)


def prepare(source, rows, target, at, transpose, n):
    x = source[pl.ds(rows, n), :]
    hi, lo = split(x.T if transpose else x)
    target[pl.ds(at, n), 0:n] = hi
    target[pl.ds(at, n), n : 2 * n] = lo


def first_stage(ops, start, count, weight, held, column, n):
    for c in range(0, count, BATCH):
        size = min(BATCH, count - c)
        got = dot(ops[start + c * n : start + (c + size) * n, :], weight)
        got = got[:, 0:n] + got[:, n : 2 * n]
        hi, lo = split(got)
        for part in range(size):
            lanes = column + (c + part) * n
            held[0:n, lanes : lanes + n] = hi[part * n : (part + 1) * n]
            held[n : 2 * n, lanes : lanes + n] = lo[part * n : (part + 1) * n]


def second_stage(held, column, count, ops, start, n):
    got = dot(held[:, column : column + count * n], ops[start : start + count * n, :])
    return (got[0:n, 0:n] + got[0:n, n : 2 * n]) + (got[n : 2 * n, 0:n] + got[n : 2 * n, n : 2 * n])


def extend(ops, weight, rows, out, scale, start, count, n):
    got = dot(ops[start : start + count * n, :], weight)
    got = got[:, 0:n] + got[:, n : 2 * n]
    hi, lo = split(got)
    tops = [hi[c * n : (c + 1) * n] for c in range(count)]
    lows = [lo[c * n : (c + 1) * n] for c in range(count)]
    wide = jnp.concatenate([jnp.concatenate(tops, 1), jnp.concatenate(lows, 1)], 0)
    done = dot(rows, wide)
    done = (done[0:n] + done[n:]) * scale
    for c in range(count):
        out[start + c * n : start + (c + 1) * n, :] = done[:, c * n : (c + 1) * n]


def kernel(
    nseg, nblk, ndiag, nhop, n,
    size_ref, rank_ref, two_ref, dl_ref, dr_ref, hl_ref, hr_ref,
    state_ref, lb_ref, rb_ref, energy_ref,
    xl, yr, far_x, far_y, state_v, lb_v, rb_v, a2, at2, b2, bt2, fx2, fy2, held,
    v_buf, c_buf, rv, rc, kept, far_kept, sums,
    load_sem, v_send, v_recv, c_send, c_recv, x_send, x_recv, k_send, k_recv, s_send, s_recv, out_sem,
):
    s = lax.axis_index("seg")
    q = lax.axis_index("blk")
    nch = ndiag + nhop
    small = ndiag * n

    loads = [
        pltpu.make_async_copy(src, dst, load_sem.at[i])
        for i, (src, dst) in enumerate(
            (
                (two_ref, c_buf.at[ITERS]),
                (hl_ref, xl.at[pl.ds(small, nhop * n)]),
                (hr_ref, yr.at[pl.ds(small, nhop * n)]),
                (dl_ref, xl.at[pl.ds(0, small)]),
                (dr_ref, yr.at[pl.ds(0, small)]),
            )
        )
    ]
    for load in loads:
        load.start()

    def per_segment(action):
        action(0)
        pl.when(s < nseg - 1)(lambda: action(1))
        pl.when(s > 0)(lambda: action(-1))

    def per_peer(step, action):
        def body(j, carry):
            action(lax.rem(q + j, nblk), j)
            return carry

        lax.fori_loop(1 if step == 0 else 0, nblk, body, 0, unroll=nblk <= 8)

    barrier = pltpu.get_barrier_semaphore()

    def greet(step):
        per_peer(
            step,
            lambda peer, j: pl.semaphore_signal(
                barrier, inc=1, device_id={"seg": s + step, "blk": peer}, device_id_type=MESH
            ),
        )

    per_segment(greet)

    @pl.when(q == 0)
    def _():
        rv[...] = jnp.zeros_like(rv)

    @pl.when(q == nblk - 1)
    def _():
        rc[...] = jnp.zeros_like(rc)

    size = size_ref[0, 0]
    count = jnp.minimum(rank_ref[0, 0], size)
    row_at = lax.broadcasted_iota(jnp.int32, (n, n), 0)
    col_at = lax.broadcasted_iota(jnp.int32, (n, n), 1)
    live = jnp.where(jnp.maximum(row_at, col_at) < size, 1.0, 0.0).astype(f32)
    col_live = jnp.where(col_at < count, 1.0, 0.0).astype(f32)

    loads[0].wait()
    v_buf[0] = live * c_buf[ITERS]

    groups = 1 + jnp.minimum(s, 1) + jnp.minimum(nseg - 1 - s, 1)
    pl.semaphore_wait(barrier, groups * nblk - 1)

    def remote(src, dst, send, recv, where):
        return pltpu.make_async_remote_copy(
            src_ref=src, dst_ref=dst, send_sem=send, recv_sem=recv,
            device_id=where, device_id_type=MESH,
        )

    def send_v(k):
        return remote(v_buf.at[k], rv.at[k], v_send.at[k], v_recv.at[k], {"seg": s, "blk": q + 1})

    def send_c(k):
        return remote(c_buf.at[k], rc.at[k], c_send.at[k], c_recv.at[k], {"seg": s, "blk": q - 1})

    up, down = {"seg": s + 1, "blk": q}, {"seg": s - 1, "blk": q}
    half = nhop // 2 * n
    chunks = [(small, half, 1), (small + half, nhop * n - half, 1), (0, small, 0)]

    def environment(refs, far, first, where):
        return [
            remote(
                refs[hop].at[pl.ds(start - small * hop, rows)],
                far.at[pl.ds(start, rows)],
                x_send.at[first + i], x_recv.at[first + i], where,
            )
            for i, (start, rows, hop) in enumerate(chunks)
        ]

    to_up = environment((dl_ref, hl_ref), far_x, 0, up)
    to_down = environment((dr_ref, hr_ref), far_y, 3, down)
    kept_up = remote(kept, far_kept.at[0], k_send.at[0], k_recv.at[0], up)
    kept_down = remote(kept, far_kept.at[1], k_send.at[1], k_recv.at[1], down)

    has_next, has_previous = q < nblk - 1, q > 0
    has_up, has_down = s < nseg - 1, s > 0

    pl.when(has_next)(lambda: send_v(0).start())

    @pl.when(has_up)
    def _():
        for copy in to_up:
            copy.start()

    @pl.when(has_down)
    def _():
        for copy in to_down:
            copy.start()

    loads[1].wait()
    loads[2].wait()
    for h in range(nhop):
        at = small + h * n
        prepare(xl, at, at2, h * n, True, n)
        prepare(yr, at, b2, h * n, False, n)

    def carried(k):
        first_stage(at2, 0, nhop, stationary(v_buf[k]), held, 0, n)
        c_buf[k] = second_stage(held, 0, nhop, b2, 0, n)
        pl.when(has_previous)(lambda: send_c(k).start())

    def finish(k):
        first_stage(a2, 0, ndiag, stationary(v_buf[k]), held, 0, n)
        pl.when(has_previous)(lambda: send_v(k).wait_recv())
        first_stage(a2, small, nhop, stationary(rv[k]), held, small, n)
        own = second_stage(held, 0, nch, bt2, 0, n)
        pl.when(has_next)(lambda: send_c(k).wait_recv())
        applied = live * (own + rc[k])
        vector = spectral_shift * v_buf[k] - applied
        v_buf[k + 1] = vector
        return applied, vector

    carried(0)
    loads[3].wait()
    loads[4].wait()
    for c in range(nch):
        prepare(xl, c * n, a2, c * n, False, n)
        prepare(yr, c * n, bt2, c * n, True, n)
    finish(0)
    pl.when(has_next)(lambda: send_v(1).start())

    def middle(k, carry):
        carried(k)
        finish(k)
        pl.when(has_next)(lambda: send_v(k + 1).start())
        return carry

    lax.fori_loop(1, ITERS - 1, middle, 0)
    carried(ITERS - 1)
    applied, vector = finish(ITERS - 1)
    last = v_buf[ITERS - 1]
    kept[...] = vector * col_live
    pl.when(has_up)(lambda: kept_up.start())
    pl.when(has_down)(lambda: kept_down.start())

    def rowsum(x):
        return jnp.sum(x, 0, keepdims=True)

    row8 = lax.broadcasted_iota(jnp.int32, (8, n), 0)
    tile = jnp.where(row8 == 0, rowsum(last * applied), 0.0)
    tile = jnp.where(row8 == 1, rowsum(last * last), tile)
    tile = jnp.where(row8 == 2, rowsum(vector * vector), tile)
    tile = jnp.where(row8 == 3, size.astype(f32) * (1.0 / n), tile)
    sums[1, q] = tile

    def sum_copy(step, peer, j):
        group = 1 - step
        return remote(
            sums.at[1, q], sums.at[group, q], s_send.at[group, j], s_recv.at[group, q],
            {"seg": s + step, "blk": peer},
        )

    def sum_arrival(group, peer):
        return remote(
            sums.at[1, q], sums.at[group, peer], s_send.at[group, 0], s_recv.at[group, peer],
            {"seg": s, "blk": peer},
        )

    per_segment(lambda step: per_peer(step, lambda peer, j: sum_copy(step, peer, j).start()))

    def totals(group):
        step = 0 if group == 1 else 1
        per_peer(step, lambda peer, j: sum_arrival(group, peer).wait_recv())
        total = sums[group, 0]
        for j in range(1, nblk):
            total = total + sums[group, j]
        return jnp.sum(total, 1, keepdims=True)

    def norm(total):
        return jnp.sqrt(total[3:4] * n / total[2:3])

    own = totals(1)
    state_v[...] = vector * norm(own)
    state_out = pltpu.make_async_copy(state_v, state_ref, out_sem.at[6])
    state_out.start()
    energy_ref[...] = own[0:1] / own[1:2]
    scale = 1.0 / jnp.sqrt(f32(n))

    def outgoing(side):
        held_out, ref = ((lb_v, lb_ref), (rb_v, rb_ref))[side]
        return [
            pltpu.make_async_copy(
                held_out.at[pl.ds(start, rows)], ref.at[pl.ds(start, rows)],
                out_sem.at[3 * side + i],
            )
            for i, (start, rows, _) in enumerate(chunks)
        ]

    def extend_side(side):
        far, ops, out, copies, arrival = (
            (far_x, fx2, lb_v, to_up, kept_up),
            (far_y, fy2, rb_v, to_down, kept_down),
        )[side]
        for i, (start, rows, _) in enumerate(chunks):
            copies[i].wait_recv()
            for at in range(start, start + rows, n):
                prepare(far, at, ops, at, side == 1, n)
            if i == 0:
                arrival.wait_recv()
                k = far_kept[side] * norm(totals(2 * side))
                first, second = (k.T, k) if side else (k, k.T)
                weight, streams = stationary(first), streamed(second)
            extend(ops, weight, streams, out, scale, start, rows // n, n)
            outgoing(side)[i].start()

    def clear(side):
        out = (lb_v, rb_v)[side]
        out[...] = jnp.zeros_like(out)
        for copy in outgoing(side):
            copy.start()

    even = lax.rem(s, 2) == 0
    pl.when(s == 0)(lambda: clear(0))
    pl.when(s == nseg - 1)(lambda: clear(1))
    pl.when(jnp.logical_and(even, has_up))(lambda: extend_side(1))
    pl.when(has_down)(lambda: extend_side(0))
    pl.when(jnp.logical_and(jnp.logical_not(even), has_up))(lambda: extend_side(1))

    @pl.when(has_next)
    def _():
        for k in range(ITERS):
            send_v(k).wait_send()

    @pl.when(has_previous)
    def _():
        for k in range(ITERS):
            send_c(k).wait_send()

    @pl.when(has_up)
    def _():
        for copy in to_up + [kept_up]:
            copy.wait_send()

    @pl.when(has_down)
    def _():
        for copy in to_down + [kept_down]:
            copy.wait_send()

    per_segment(lambda step: per_peer(step, lambda peer, j: sum_copy(step, peer, j).wait_send()))
    for copy in outgoing(0) + outgoing(1) + [state_out]:
        copy.wait()


def write_out(*refs):
    sem = refs[6]
    copies = []
    for i in range(3):
        rows = refs[i].shape[0] // 2
        for at in (0, rows):
            part = pl.ds(at, rows)
            copies.append(
                pltpu.make_async_copy(refs[i].at[part], refs[3 + i].at[part], sem.at[len(copies)])
            )
    for copy in copies:
        copy.start()
    for copy in copies:
        copy.wait()


def shards(nseg, nblk, two_site, diag_left, diag_right, hop_left, hop_right, sector_sizes, ranks):
    n = two_site.shape[2]
    ndiag, nhop = diag_left.shape[2], hop_left.shape[2]
    nch = ndiag + nhop
    smem = pl.BlockSpec(memory_space=pltpu.SMEM)
    vmem = pl.BlockSpec(memory_space=pltpu.VMEM)
    hbm = pl.BlockSpec(memory_space=pltpu.HBM)
    dma = pltpu.SemaphoreType.DMA
    state, left, right, energy = pl.pallas_call(
        functools.partial(kernel, nseg, nblk, ndiag, nhop, n),
        out_shape=(
            jax.ShapeDtypeStruct((n, n), f32),
            jax.ShapeDtypeStruct((nch * n, n), f32),
            jax.ShapeDtypeStruct((nch * n, n), f32),
            jax.ShapeDtypeStruct((1, 1), f32),
        ),
        in_specs=[smem, smem] + [hbm] * 5,
        out_specs=(hbm, hbm, hbm, vmem),
        scratch_shapes=[
            pltpu.VMEM((nch * n, n), f32),
            pltpu.VMEM((nch * n, n), f32),
            pltpu.VMEM((nch * n, n), f32),
            pltpu.VMEM((nch * n, n), f32),
            pltpu.VMEM((n, n), f32),
            pltpu.VMEM((nch * n, n), f32),
            pltpu.VMEM((nch * n, n), f32),
            pltpu.VMEM((nch * n, 2 * n), bf16),
            pltpu.VMEM((nhop * n, 2 * n), bf16),
            pltpu.VMEM((nhop * n, 2 * n), bf16),
            pltpu.VMEM((nch * n, 2 * n), bf16),
            pltpu.VMEM((nch * n, 2 * n), bf16),
            pltpu.VMEM((nch * n, 2 * n), bf16),
            pltpu.VMEM((2 * n, nch * n), bf16),
            pltpu.VMEM((ITERS + 1, n, n), f32),
            pltpu.VMEM((ITERS + 1, n, n), f32),
            pltpu.VMEM((ITERS, n, n), f32),
            pltpu.VMEM((ITERS, n, n), f32),
            pltpu.VMEM((n, n), f32),
            pltpu.VMEM((2, n, n), f32),
            pltpu.VMEM((3, nblk, 8, n), f32),
            dma((5,)),
            dma((ITERS,)),
            dma((ITERS,)),
            dma((ITERS,)),
            dma((ITERS,)),
            dma((6,)),
            dma((6,)),
            dma((2,)),
            dma((2,)),
            dma((3, nblk)),
            dma((3, nblk)),
            dma((7,)),
        ],
        compiler_params=pltpu.CompilerParams(
            collective_id=0, has_side_effects=True, vmem_limit_bytes=57 * 1024 * 1024
        ),
        name="solve",
    )(
        sector_sizes, ranks,
        two_site.reshape(n, n),
        diag_left.reshape(ndiag * n, n),
        diag_right.reshape(ndiag * n, n),
        hop_left.reshape(nhop * n, n),
        hop_right.reshape(nhop * n, n),
    )
    state, left, right = pl.pallas_call(
        write_out,
        out_shape=tuple(jax.ShapeDtypeStruct(x.shape, f32) for x in (state, left, right)),
        in_specs=[hbm] * 3,
        out_specs=(hbm,) * 3,
        scratch_shapes=[dma((6,))],
        compiler_params=pltpu.CompilerParams(vmem_limit_bytes=57 * 1024 * 1024),
        name="write_out",
    )(state, left, right)
    return (
        state.reshape(1, 1, n, n),
        left.reshape(1, 1, nch, n, n),
        right.reshape(1, 1, nch, n, n),
        energy.reshape(1),
    )


def solution(mesh):
    nseg, nblk = mesh.shape["seg"], mesh.shape["blk"]
    return jax.shard_map(
        functools.partial(shards, nseg, nblk),
        mesh=mesh,
        in_specs=(
            P("seg", "blk", None, None),
            P("seg", "blk", None, None, None),
            P("seg", "blk", None, None, None),
            P("seg", "blk", None, None, None),
            P("seg", "blk", None, None, None),
            P("seg", "blk"),
            P("seg", "blk"),
        ),
        out_specs=(
            P("seg", "blk", None, None),
            P("seg", "blk", None, None, None),
            P("seg", "blk", None, None, None),
            P("seg"),
        ),
        check_vma=False,
    )
```

```python
import functools

import jax
import jax.numpy as jnp
from jax import lax
from jax.experimental import pallas as pl
from jax.experimental.pallas import tpu as pltpu
from jax.sharding import PartitionSpec as P

ITERS = 4
BATCH = 8
MESH = pl.DeviceIdType.MESH
f32 = jnp.float32
bf16 = jnp.bfloat16
spectral_shift = 20.0


def split(x):
    hi = x.astype(bf16)
    lo = (x - hi.astype(f32)).astype(bf16)
    return hi, lo


def stationary(x):
    hi, lo = split(x)
    top = jnp.concatenate([hi, lo], 1)
    low = jnp.concatenate([hi, jnp.zeros_like(hi)], 1)
    return jnp.concatenate([top, low], 0)


def streamed(x):
    hi, lo = split(x)
    top = jnp.concatenate([hi, hi], 1)
    low = jnp.concatenate([lo, jnp.zeros_like(lo)], 1)
    return jnp.concatenate([top, low], 0)


def dot(a, b):
    return jnp.dot(a, b, preferred_element_type=f32)


def prepare(source, rows, target, at, transpose, n):
    x = source[pl.ds(rows, n), :]
    hi, lo = split(x.T if transpose else x)
    target[pl.ds(at, n), 0:n] = hi
    target[pl.ds(at, n), n : 2 * n] = lo


def first_stage(ops, start, count, weight, held, column, n):
    for c in range(0, count, BATCH):
        size = min(BATCH, count - c)
        got = dot(ops[start + c * n : start + (c + size) * n, :], weight)
        got = got[:, 0:n] + got[:, n : 2 * n]
        hi, lo = split(got)
        for part in range(size):
            lanes = column + (c + part) * n
            held[0:n, lanes : lanes + n] = hi[part * n : (part + 1) * n]
            held[n : 2 * n, lanes : lanes + n] = lo[part * n : (part + 1) * n]


def second_stage(held, column, count, ops, start, n):
    got = dot(held[:, column : column + count * n], ops[start : start + count * n, :])
    return (got[0:n, 0:n] + got[0:n, n : 2 * n]) + (got[n : 2 * n, 0:n] + got[n : 2 * n, n : 2 * n])


def extend(ops, weight, rows, out, scale, start, count, n):
    got = dot(ops[start : start + count * n, :], weight)
    got = got[:, 0:n] + got[:, n : 2 * n]
    hi, lo = split(got)
    tops = [hi[c * n : (c + 1) * n] for c in range(count)]
    lows = [lo[c * n : (c + 1) * n] for c in range(count)]
    wide = jnp.concatenate([jnp.concatenate(tops, 1), jnp.concatenate(lows, 1)], 0)
    done = dot(rows, wide)
    done = (done[0:n] + done[n:]) * scale
    for c in range(count):
        out[start + c * n : start + (c + 1) * n, :] = done[:, c * n : (c + 1) * n]


def kernel(
    nseg, nblk, ndiag, nhop, n,
    size_ref, rank_ref, two_ref, dl_ref, dr_ref, hl_ref, hr_ref,
    state_ref, lb_ref, rb_ref, energy_ref,
    xl, yr, far_x, far_y, state_v, lb_v, rb_v, a2, at2, b2, bt2, fx2, fy2, held,
    v_buf, c_buf, rv, rc, kept, far_kept, sums,
    load_sem, v_send, v_recv, c_send, c_recv, x_send, x_recv, k_send, k_recv, s_send, s_recv, out_sem, relay, r_send, r_recv,
):
    s = lax.axis_index("seg")
    q = lax.axis_index("blk")
    nch = ndiag + nhop
    small = ndiag * n

    loads = [
        pltpu.make_async_copy(src, dst, load_sem.at[i])
        for i, (src, dst) in enumerate(
            (
                (two_ref, c_buf.at[ITERS]),
                (hl_ref, xl.at[pl.ds(small, nhop * n)]),
                (hr_ref, yr.at[pl.ds(small, nhop * n)]),
                (dl_ref, xl.at[pl.ds(0, small)]),
                (dr_ref, yr.at[pl.ds(0, small)]),
            )
        )
    ]
    for load in loads:
        load.start()

    def per_segment(action):
        action(0)
        pl.when(s < nseg - 1)(lambda: action(1))
        pl.when(s > 0)(lambda: action(-1))

    def per_peer(step, action):
        def body(j, carry):
            action(lax.rem(q + j, nblk), j)
            return carry

        lax.fori_loop(1 if step == 0 else 0, nblk, body, 0, unroll=nblk <= 8)

    barrier = pltpu.get_barrier_semaphore()

    def greet(step):
        per_peer(
            step,
            lambda peer, j: pl.semaphore_signal(
                barrier, inc=1, device_id={"seg": s + step, "blk": peer}, device_id_type=MESH
            ),
        )

    per_segment(greet)

    below, above = nseg // 2 - 1, nseg // 2
    relays = ((below, nseg - 1, above), (above, 0, below))

    def on_relay(action):
        for origin, via, target in relays:
            action(origin, via, target)

    def greet_relay(origin, via, target):
        for first, second in ((origin, via), (via, origin), (via, target), (target, via)):
            @pl.when(s == first)
            def _(second=second):
                pl.semaphore_signal(
                    barrier, inc=1, device_id={"seg": second, "blk": q}, device_id_type=MESH
                )

    on_relay(greet_relay)

    @pl.when(q == 0)
    def _():
        rv[...] = jnp.zeros_like(rv)

    @pl.when(q == nblk - 1)
    def _():
        rc[...] = jnp.zeros_like(rc)

    size = size_ref[0, 0]
    count = jnp.minimum(rank_ref[0, 0], size)
    row_at = lax.broadcasted_iota(jnp.int32, (n, n), 0)
    col_at = lax.broadcasted_iota(jnp.int32, (n, n), 1)
    live = jnp.where(jnp.maximum(row_at, col_at) < size, 1.0, 0.0).astype(f32)
    col_live = jnp.where(col_at < count, 1.0, 0.0).astype(f32)

    loads[0].wait()
    v_buf[0] = live * c_buf[ITERS]

    groups = 1 + jnp.minimum(s, 1) + jnp.minimum(nseg - 1 - s, 1)
    others = 0
    for place in (0, below, above, nseg - 1):
        others = others + 2 * (1 - jnp.minimum(jnp.maximum(s - place, place - s), 1))
    pl.semaphore_wait(barrier, groups * nblk - 1 + others)

    def remote(src, dst, send, recv, where):
        return pltpu.make_async_remote_copy(
            src_ref=src, dst_ref=dst, send_sem=send, recv_sem=recv,
            device_id=where, device_id_type=MESH,
        )

    def send_v(k):
        return remote(v_buf.at[k], rv.at[k], v_send.at[k], v_recv.at[k], {"seg": s, "blk": q + 1})

    def send_c(k):
        return remote(c_buf.at[k], rc.at[k], c_send.at[k], c_recv.at[k], {"seg": s, "blk": q - 1})

    up, down = {"seg": s + 1, "blk": q}, {"seg": s - 1, "blk": q}
    half = nhop // 2 * n
    chunks = [(small, half, 1), (small + half, nhop * n - half, 1), (0, small, 0)]

    def environment(refs, far, first, where):
        return [
            remote(
                refs[hop].at[pl.ds(start - small * hop, rows)],
                far.at[pl.ds(start, rows)],
                x_send.at[first + i], x_recv.at[first + i], where,
            )
            for i, (start, rows, hop) in enumerate(chunks)
        ]

    to_up = environment((dl_ref, hl_ref), far_x, 0, up)
    to_down = environment((dr_ref, hr_ref), far_y, 3, down)
    kept_up = remote(kept, far_kept.at[0], k_send.at[0], k_recv.at[0], up)
    kept_down = remote(kept, far_kept.at[1], k_send.at[1], k_recv.at[1], down)

    has_next, has_previous = q < nblk - 1, q > 0
    has_up, has_down = s < nseg - 1, s > 0

    pl.when(has_next)(lambda: send_v(0).start())

    def to_relay(origin, via, target):
        start, rows, _ = chunks[1]
        source = hl_ref if origin < target else hr_ref
        return remote(
            source.at[pl.ds(start - small, rows)], relay, r_send.at[0], r_recv.at[0],
            {"seg": via, "blk": q},
        )

    def from_relay(origin, via, target):
        start, rows, _ = chunks[1]
        far, i = (far_x, 1) if origin < target else (far_y, 4)
        return remote(
            relay, far.at[pl.ds(start, rows)], r_send.at[1], x_recv.at[i],
            {"seg": target, "blk": q},
        )

    def send_environments(action):
        on_relay(lambda *way: pl.when(s == way[0])(lambda: action(to_relay(*way))))
        for copies, some, middle in ((to_up, has_up, below), (to_down, has_down, above)):
            pl.when(some)(lambda: action(copies[0]))
            pl.when(jnp.logical_and(some, s != middle))(lambda: action(copies[1]))
            pl.when(some)(lambda: action(copies[2]))

    def pass_on(*way):
        @pl.when(s == way[1])
        def _():
            to_relay(*way).wait_recv()
            from_relay(*way).start()

    send_environments(lambda copy: copy.start())

    loads[1].wait()
    loads[2].wait()
    for h in range(nhop):
        at = small + h * n
        prepare(xl, at, at2, h * n, True, n)
        prepare(yr, at, b2, h * n, False, n)

    def carried(k):
        first_stage(at2, 0, nhop, stationary(v_buf[k]), held, 0, n)
        c_buf[k] = second_stage(held, 0, nhop, b2, 0, n)
        pl.when(has_previous)(lambda: send_c(k).start())

    def finish(k):
        first_stage(a2, 0, ndiag, stationary(v_buf[k]), held, 0, n)
        pl.when(has_previous)(lambda: send_v(k).wait_recv())
        first_stage(a2, small, nhop, stationary(rv[k]), held, small, n)
        own = second_stage(held, 0, nch, bt2, 0, n)
        pl.when(has_next)(lambda: send_c(k).wait_recv())
        applied = live * (own + rc[k])
        vector = spectral_shift * v_buf[k] - applied
        v_buf[k + 1] = vector
        return applied, vector

    carried(0)
    loads[3].wait()
    loads[4].wait()
    for c in range(nch):
        prepare(xl, c * n, a2, c * n, False, n)
        prepare(yr, c * n, bt2, c * n, True, n)
    finish(0)
    pl.when(has_next)(lambda: send_v(1).start())

    def middle(k, carry):
        carried(k)
        finish(k)
        pl.when(has_next)(lambda: send_v(k + 1).start())
        pl.when(k == 1)(lambda: on_relay(pass_on))
        return carry

    lax.fori_loop(1, ITERS - 1, middle, 0)
    carried(ITERS - 1)
    applied, vector = finish(ITERS - 1)
    last = v_buf[ITERS - 1]
    kept[...] = vector * col_live
    pl.when(has_up)(lambda: kept_up.start())
    pl.when(has_down)(lambda: kept_down.start())

    def rowsum(x):
        return jnp.sum(x, 0, keepdims=True)

    row8 = lax.broadcasted_iota(jnp.int32, (8, n), 0)
    tile = jnp.where(row8 == 0, rowsum(last * applied), 0.0)
    tile = jnp.where(row8 == 1, rowsum(last * last), tile)
    tile = jnp.where(row8 == 2, rowsum(vector * vector), tile)
    tile = jnp.where(row8 == 3, size.astype(f32) * (1.0 / n), tile)
    sums[1, q] = tile

    def sum_copy(step, peer, j):
        group = 1 - step
        return remote(
            sums.at[1, q], sums.at[group, q], s_send.at[group, j], s_recv.at[group, q],
            {"seg": s + step, "blk": peer},
        )

    def sum_arrival(group, peer):
        return remote(
            sums.at[1, q], sums.at[group, peer], s_send.at[group, 0], s_recv.at[group, peer],
            {"seg": s, "blk": peer},
        )

    per_segment(lambda step: per_peer(step, lambda peer, j: sum_copy(step, peer, j).start()))

    def totals(group):
        step = 0 if group == 1 else 1
        per_peer(step, lambda peer, j: sum_arrival(group, peer).wait_recv())
        total = sums[group, 0]
        for j in range(1, nblk):
            total = total + sums[group, j]
        return jnp.sum(total, 1, keepdims=True)

    def norm(total):
        return jnp.sqrt(total[3:4] * n / total[2:3])

    own = totals(1)
    state_v[...] = vector * norm(own)
    state_out = pltpu.make_async_copy(state_v, state_ref, out_sem.at[6])
    state_out.start()
    energy_ref[...] = own[0:1] / own[1:2]
    scale = 1.0 / jnp.sqrt(f32(n))

    def outgoing(side):
        held_out, ref = ((lb_v, lb_ref), (rb_v, rb_ref))[side]
        return [
            pltpu.make_async_copy(
                held_out.at[pl.ds(start, rows)], ref.at[pl.ds(start, rows)],
                out_sem.at[3 * side + i],
            )
            for i, (start, rows, _) in enumerate(chunks)
        ]

    def extend_side(side):
        far, ops, out, copies, arrival = (
            (far_x, fx2, lb_v, to_up, kept_up),
            (far_y, fy2, rb_v, to_down, kept_down),
        )[side]
        for i, (start, rows, _) in enumerate(chunks):
            copies[i].wait_recv()
            for at in range(start, start + rows, n):
                prepare(far, at, ops, at, side == 1, n)
            if i == 0:
                arrival.wait_recv()
                k = far_kept[side] * norm(totals(2 * side))
                first, second = (k.T, k) if side else (k, k.T)
                weight, streams = stationary(first), streamed(second)
            extend(ops, weight, streams, out, scale, start, rows // n, n)
            outgoing(side)[i].start()

    def clear(side):
        out = (lb_v, rb_v)[side]
        out[...] = jnp.zeros_like(out)
        for copy in outgoing(side):
            copy.start()

    even = lax.rem(s, 2) == 0
    pl.when(s == 0)(lambda: clear(0))
    pl.when(s == nseg - 1)(lambda: clear(1))
    pl.when(jnp.logical_and(even, has_up))(lambda: extend_side(1))
    pl.when(has_down)(lambda: extend_side(0))
    pl.when(jnp.logical_and(jnp.logical_not(even), has_up))(lambda: extend_side(1))

    @pl.when(has_next)
    def _():
        for k in range(ITERS):
            send_v(k).wait_send()

    @pl.when(has_previous)
    def _():
        for k in range(ITERS):
            send_c(k).wait_send()

    send_environments(lambda copy: copy.wait_send())
    on_relay(lambda *way: pl.when(s == way[1])(lambda: from_relay(*way).wait_send()))
    pl.when(has_up)(lambda: kept_up.wait_send())
    pl.when(has_down)(lambda: kept_down.wait_send())
    per_segment(lambda step: per_peer(step, lambda peer, j: sum_copy(step, peer, j).wait_send()))
    for copy in outgoing(0) + outgoing(1) + [state_out]:
        copy.wait()


def write_out(*refs):
    loaded, sems = refs[6:9], refs[9]
    copies = []
    for i in range(3):
        rows = refs[i].shape[0]
        step = max(rows // 3, 128)
        for at in range(0, rows, step):
            part = pl.ds(at, min(step, rows - at))
            j = len(copies)
            copies.append(
                (
                    pltpu.make_async_copy(refs[i].at[part], loaded[i].at[part], sems.at[0, j]),
                    pltpu.make_async_copy(loaded[i].at[part], refs[3 + i].at[part], sems.at[1, j]),
                )
            )
    for load, _ in copies:
        load.start()
    for load, store in copies:
        load.wait()
        store.start()
    for _, store in copies:
        store.wait()


def shards(nseg, nblk, two_site, diag_left, diag_right, hop_left, hop_right, sector_sizes, ranks):
    n = two_site.shape[2]
    ndiag, nhop = diag_left.shape[2], hop_left.shape[2]
    nch = ndiag + nhop
    smem = pl.BlockSpec(memory_space=pltpu.SMEM)
    vmem = pl.BlockSpec(memory_space=pltpu.VMEM)
    hbm = pl.BlockSpec(memory_space=pltpu.HBM)
    dma = pltpu.SemaphoreType.DMA
    state, left, right, energy = pl.pallas_call(
        functools.partial(kernel, nseg, nblk, ndiag, nhop, n),
        out_shape=(
            jax.ShapeDtypeStruct((n, n), f32),
            jax.ShapeDtypeStruct((nch * n, n), f32),
            jax.ShapeDtypeStruct((nch * n, n), f32),
            jax.ShapeDtypeStruct((1, 1), f32),
        ),
        in_specs=[smem, smem] + [hbm] * 5,
        out_specs=(hbm, hbm, hbm, vmem),
        scratch_shapes=[
            pltpu.VMEM((nch * n, n), f32),
            pltpu.VMEM((nch * n, n), f32),
            pltpu.VMEM((nch * n, n), f32),
            pltpu.VMEM((nch * n, n), f32),
            pltpu.VMEM((n, n), f32),
            pltpu.VMEM((nch * n, n), f32),
            pltpu.VMEM((nch * n, n), f32),
            pltpu.VMEM((nch * n, 2 * n), bf16),
            pltpu.VMEM((nhop * n, 2 * n), bf16),
            pltpu.VMEM((nhop * n, 2 * n), bf16),
            pltpu.VMEM((nch * n, 2 * n), bf16),
            pltpu.VMEM((nch * n, 2 * n), bf16),
            pltpu.VMEM((nch * n, 2 * n), bf16),
            pltpu.VMEM((2 * n, nch * n), bf16),
            pltpu.VMEM((ITERS + 1, n, n), f32),
            pltpu.VMEM((ITERS + 1, n, n), f32),
            pltpu.VMEM((ITERS, n, n), f32),
            pltpu.VMEM((ITERS, n, n), f32),
            pltpu.VMEM((n, n), f32),
            pltpu.VMEM((2, n, n), f32),
            pltpu.VMEM((3, nblk, 8, n), f32),
            dma((5,)),
            dma((ITERS,)),
            dma((ITERS,)),
            dma((ITERS,)),
            dma((ITERS,)),
            dma((6,)),
            dma((6,)),
            dma((2,)),
            dma((2,)),
            dma((3, nblk)),
            dma((3, nblk)),
            dma((7,)),
            pltpu.VMEM((nhop * n - nhop // 2 * n, n), f32),
            dma((2,)),
            dma((1,)),
        ],
        compiler_params=pltpu.CompilerParams(
            collective_id=0, has_side_effects=True, vmem_limit_bytes=57 * 1024 * 1024
        ),
        name="solve",
    )(
        sector_sizes, ranks,
        two_site.reshape(n, n),
        diag_left.reshape(ndiag * n, n),
        diag_right.reshape(ndiag * n, n),
        hop_left.reshape(nhop * n, n),
        hop_right.reshape(nhop * n, n),
    )
    state, left, right = pl.pallas_call(
        write_out,
        out_shape=tuple(jax.ShapeDtypeStruct(x.shape, f32) for x in (state, left, right)),
        in_specs=[hbm] * 3,
        out_specs=(hbm,) * 3,
        scratch_shapes=[pltpu.VMEM(x.shape, f32) for x in (state, left, right)] + [dma((2, 8))],
        compiler_params=pltpu.CompilerParams(vmem_limit_bytes=57 * 1024 * 1024),
        name="write_out",
    )(state, left, right)
    return (
        state.reshape(1, 1, n, n),
        left.reshape(1, 1, nch, n, n),
        right.reshape(1, 1, nch, n, n),
        energy.reshape(1),
    )


def solution(mesh):
    nseg, nblk = mesh.shape["seg"], mesh.shape["blk"]
    return jax.shard_map(
        functools.partial(shards, nseg, nblk),
        mesh=mesh,
        in_specs=(
            P("seg", "blk", None, None),
            P("seg", "blk", None, None, None),
            P("seg", "blk", None, None, None),
            P("seg", "blk", None, None, None),
            P("seg", "blk", None, None, None),
            P("seg", "blk"),
            P("seg", "blk"),
        ),
        out_specs=(
            P("seg", "blk", None, None),
            P("seg", "blk", None, None, None),
            P("seg", "blk", None, None, None),
            P("seg"),
        ),
        check_vma=False,
    )
```

```python
import functools

import jax
import jax.numpy as jnp
from jax import lax
from jax.experimental import pallas as pl
from jax.experimental.pallas import tpu as pltpu
from jax.sharding import PartitionSpec as P

ITERS = 4
BATCH = 8
MESH = pl.DeviceIdType.MESH
f32 = jnp.float32
bf16 = jnp.bfloat16
spectral_shift = 20.0


def split(x):
    hi = x.astype(bf16)
    lo = (x - hi.astype(f32)).astype(bf16)
    return hi, lo


def stationary(x):
    hi, lo = split(x)
    top = jnp.concatenate([hi, lo], 1)
    low = jnp.concatenate([hi, jnp.zeros_like(hi)], 1)
    return jnp.concatenate([top, low], 0)


def streamed(x):
    hi, lo = split(x)
    top = jnp.concatenate([hi, hi], 1)
    low = jnp.concatenate([lo, jnp.zeros_like(lo)], 1)
    return jnp.concatenate([top, low], 0)


def dot(a, b):
    return jnp.dot(a, b, preferred_element_type=f32)


def prepare(source, rows, target, at, transpose, n):
    x = source[pl.ds(rows, n), :]
    hi, lo = split(x.T if transpose else x)
    target[pl.ds(at, n), 0:n] = hi
    target[pl.ds(at, n), n : 2 * n] = lo


def first_stage(ops, start, count, weight, held, column, n):
    for c in range(0, count, BATCH):
        size = min(BATCH, count - c)
        got = dot(ops[start + c * n : start + (c + size) * n, :], weight)
        got = got[:, 0:n] + got[:, n : 2 * n]
        hi, lo = split(got)
        for part in range(size):
            lanes = column + (c + part) * n
            held[0:n, lanes : lanes + n] = hi[part * n : (part + 1) * n]
            held[n : 2 * n, lanes : lanes + n] = lo[part * n : (part + 1) * n]


def second_stage(held, column, count, ops, start, n):
    got = dot(held[:, column : column + count * n], ops[start : start + count * n, :])
    return (got[0:n, 0:n] + got[0:n, n : 2 * n]) + (got[n : 2 * n, 0:n] + got[n : 2 * n, n : 2 * n])


def extend(ops, weight, rows, out, scale, start, count, n):
    got = dot(ops[start : start + count * n, :], weight)
    got = got[:, 0:n] + got[:, n : 2 * n]
    hi, lo = split(got)
    tops = [hi[c * n : (c + 1) * n] for c in range(count)]
    lows = [lo[c * n : (c + 1) * n] for c in range(count)]
    wide = jnp.concatenate([jnp.concatenate(tops, 1), jnp.concatenate(lows, 1)], 0)
    done = dot(rows, wide)
    done = (done[0:n] + done[n:]) * scale
    for c in range(count):
        out[start + c * n : start + (c + 1) * n, :] = done[:, c * n : (c + 1) * n]


def kernel(
    nseg, nblk, ndiag, nhop, n,
    size_ref, rank_ref, two_ref, dl_ref, dr_ref, hl_ref, hr_ref,
    state_ref, lb_ref, rb_ref, energy_ref,
    xl, yr, far_x, far_y, state_v, lb_v, rb_v, a2, at2, b2, bt2, fx2, fy2, held,
    v_buf, c_buf, rv, rc, kept, far_kept, sums,
    load_sem, v_send, v_recv, c_send, c_recv, x_send, x_recv, k_send, k_recv, s_send, s_recv, out_sem, relay, r_send, r_recv,
):
    s = lax.axis_index("seg")
    q = lax.axis_index("blk")
    nch = ndiag + nhop
    small = ndiag * n

    loads = [
        pltpu.make_async_copy(src, dst, load_sem.at[i])
        for i, (src, dst) in enumerate(
            (
                (two_ref, c_buf.at[ITERS]),
                (hl_ref, xl.at[pl.ds(small, nhop * n)]),
                (hr_ref, yr.at[pl.ds(small, nhop * n)]),
                (dl_ref, xl.at[pl.ds(0, small)]),
                (dr_ref, yr.at[pl.ds(0, small)]),
            )
        )
    ]
    for load in loads:
        load.start()

    def per_segment(action):
        action(0)
        pl.when(s < nseg - 1)(lambda: action(1))
        pl.when(s > 0)(lambda: action(-1))

    def per_peer(step, action):
        def body(j, carry):
            action(lax.rem(q + j, nblk), j)
            return carry

        lax.fori_loop(1 if step == 0 else 0, nblk, body, 0, unroll=nblk <= 8)

    barrier = pltpu.get_barrier_semaphore()

    def greet(step):
        per_peer(
            step,
            lambda peer, j: pl.semaphore_signal(
                barrier, inc=1, device_id={"seg": s + step, "blk": peer}, device_id_type=MESH
            ),
        )

    per_segment(greet)

    below, above = nseg // 2 - 1, nseg // 2
    relays = ((below, nseg - 1, above), (above, 0, below))

    def on_relay(action):
        for origin, via, target in relays:
            action(origin, via, target)

    def greet_relay(origin, via, target):
        for first, second in ((origin, via), (via, origin), (via, target), (target, via)):
            @pl.when(s == first)
            def _(second=second):
                pl.semaphore_signal(
                    barrier, inc=1, device_id={"seg": second, "blk": q}, device_id_type=MESH
                )

    on_relay(greet_relay)

    @pl.when(q == 0)
    def _():
        rv[...] = jnp.zeros_like(rv)

    @pl.when(q == nblk - 1)
    def _():
        rc[...] = jnp.zeros_like(rc)

    size = size_ref[0, 0]
    count = jnp.minimum(rank_ref[0, 0], size)
    row_at = lax.broadcasted_iota(jnp.int32, (n, n), 0)
    col_at = lax.broadcasted_iota(jnp.int32, (n, n), 1)
    live = jnp.where(jnp.maximum(row_at, col_at) < size, 1.0, 0.0).astype(f32)
    col_live = jnp.where(col_at < count, 1.0, 0.0).astype(f32)

    loads[0].wait()
    v_buf[0] = live * c_buf[ITERS]

    loads[1].wait()
    loads[2].wait()
    for h in range(nhop):
        at = small + h * n
        prepare(xl, at, at2, h * n, True, n)
        prepare(yr, at, b2, h * n, False, n)

    groups = 1 + jnp.minimum(s, 1) + jnp.minimum(nseg - 1 - s, 1)
    others = 0
    for place in (0, below, above, nseg - 1):
        others = others + 2 * (1 - jnp.minimum(jnp.maximum(s - place, place - s), 1))
    pl.semaphore_wait(barrier, groups * nblk - 1 + others)

    def remote(src, dst, send, recv, where):
        return pltpu.make_async_remote_copy(
            src_ref=src, dst_ref=dst, send_sem=send, recv_sem=recv,
            device_id=where, device_id_type=MESH,
        )

    def send_v(k):
        return remote(v_buf.at[k], rv.at[k], v_send.at[k], v_recv.at[k], {"seg": s, "blk": q + 1})

    def send_c(k):
        return remote(c_buf.at[k], rc.at[k], c_send.at[k], c_recv.at[k], {"seg": s, "blk": q - 1})

    up, down = {"seg": s + 1, "blk": q}, {"seg": s - 1, "blk": q}
    half = nhop // 2 * n
    chunks = [(small, half, 1), (small + half, nhop * n - half, 1), (0, small, 0)]

    def environment(refs, far, first, where):
        return [
            remote(
                refs[hop].at[pl.ds(start - small * hop, rows)],
                far.at[pl.ds(start, rows)],
                x_send.at[first + i], x_recv.at[first + i], where,
            )
            for i, (start, rows, hop) in enumerate(chunks)
        ]

    to_up = environment((dl_ref, hl_ref), far_x, 0, up)
    to_down = environment((dr_ref, hr_ref), far_y, 3, down)
    kept_up = remote(kept, far_kept.at[0], k_send.at[0], k_recv.at[0], up)
    kept_down = remote(kept, far_kept.at[1], k_send.at[1], k_recv.at[1], down)

    has_next, has_previous = q < nblk - 1, q > 0
    has_up, has_down = s < nseg - 1, s > 0

    pl.when(has_next)(lambda: send_v(0).start())

    def to_relay(origin, via, target):
        start, rows, _ = chunks[1]
        source = hl_ref if origin < target else hr_ref
        return remote(
            source.at[pl.ds(start - small, rows)], relay, r_send.at[0], r_recv.at[0],
            {"seg": via, "blk": q},
        )

    def from_relay(origin, via, target):
        start, rows, _ = chunks[1]
        far, i = (far_x, 1) if origin < target else (far_y, 4)
        return remote(
            relay, far.at[pl.ds(start, rows)], r_send.at[1], x_recv.at[i],
            {"seg": target, "blk": q},
        )

    def send_environments(action):
        on_relay(lambda *way: pl.when(s == way[0])(lambda: action(to_relay(*way))))
        for copies, some, middle in ((to_up, has_up, below), (to_down, has_down, above)):
            pl.when(some)(lambda: action(copies[0]))
            pl.when(jnp.logical_and(some, s != middle))(lambda: action(copies[1]))
            pl.when(some)(lambda: action(copies[2]))

    def pass_on(*way):
        @pl.when(s == way[1])
        def _():
            to_relay(*way).wait_recv()
            from_relay(*way).start()

    send_environments(lambda copy: copy.start())

    def carried(k):
        first_stage(at2, 0, nhop, stationary(v_buf[k]), held, 0, n)
        c_buf[k] = second_stage(held, 0, nhop, b2, 0, n)
        pl.when(has_previous)(lambda: send_c(k).start())

    def finish(k):
        first_stage(a2, 0, ndiag, stationary(v_buf[k]), held, 0, n)
        pl.when(has_previous)(lambda: send_v(k).wait_recv())
        first_stage(a2, small, nhop, stationary(rv[k]), held, small, n)
        own = second_stage(held, 0, nch, bt2, 0, n)
        pl.when(has_next)(lambda: send_c(k).wait_recv())
        applied = live * (own + rc[k])
        vector = spectral_shift * v_buf[k] - applied
        v_buf[k + 1] = vector
        return applied, vector

    carried(0)
    loads[3].wait()
    loads[4].wait()
    for c in range(nch):
        prepare(xl, c * n, a2, c * n, False, n)
        prepare(yr, c * n, bt2, c * n, True, n)
    finish(0)
    pl.when(has_next)(lambda: send_v(1).start())

    sides = ((far_x, fx2, lb_v, to_up, kept_up), (far_y, fy2, rb_v, to_down, kept_down))
    even = lax.rem(s, 2) == 0
    odd = jnp.logical_not(even)

    def prepare_side(side):
        far, ops, _, copies, _ = sides[side]
        for copy in copies:
            copy.wait_recv()
        for c in range(nch):
            prepare(far, c * n, ops, c * n, side == 1, n)

    def middle(k, carry):
        carried(k)
        finish(k)
        pl.when(has_next)(lambda: send_v(k + 1).start())
        pl.when(k == 1)(lambda: on_relay(pass_on))
        return carry

    lax.fori_loop(1, ITERS - 1, middle, 0)
    carried(ITERS - 1)
    pl.when(jnp.logical_and(even, has_up))(lambda: prepare_side(1))
    pl.when(jnp.logical_and(odd, has_down))(lambda: prepare_side(0))
    applied, vector = finish(ITERS - 1)
    last = v_buf[ITERS - 1]
    kept[...] = vector * col_live
    pl.when(has_up)(lambda: kept_up.start())
    pl.when(has_down)(lambda: kept_down.start())

    def rowsum(x):
        return jnp.sum(x, 0, keepdims=True)

    row8 = lax.broadcasted_iota(jnp.int32, (8, n), 0)
    tile = jnp.where(row8 == 0, rowsum(last * applied), 0.0)
    tile = jnp.where(row8 == 1, rowsum(last * last), tile)
    tile = jnp.where(row8 == 2, rowsum(vector * vector), tile)
    tile = jnp.where(row8 == 3, size.astype(f32) * (1.0 / n), tile)
    sums[1, q] = tile

    def sum_copy(step, peer, j):
        group = 1 - step
        return remote(
            sums.at[1, q], sums.at[group, q], s_send.at[group, j], s_recv.at[group, q],
            {"seg": s + step, "blk": peer},
        )

    def sum_arrival(group, peer):
        return remote(
            sums.at[1, q], sums.at[group, peer], s_send.at[group, 0], s_recv.at[group, peer],
            {"seg": s, "blk": peer},
        )

    per_segment(lambda step: per_peer(step, lambda peer, j: sum_copy(step, peer, j).start()))

    pl.when(jnp.logical_and(even, has_down))(lambda: prepare_side(0))
    pl.when(jnp.logical_and(odd, has_up))(lambda: prepare_side(1))

    def totals(group):
        step = 0 if group == 1 else 1
        per_peer(step, lambda peer, j: sum_arrival(group, peer).wait_recv())
        total = sums[group, 0]
        for j in range(1, nblk):
            total = total + sums[group, j]
        return jnp.sum(total, 1, keepdims=True)

    def norm(total):
        return jnp.sqrt(total[3:4] * n / total[2:3])

    own = totals(1)
    state_v[...] = vector * norm(own)
    state_out = pltpu.make_async_copy(state_v, state_ref, out_sem.at[6])
    state_out.start()
    energy_ref[...] = own[0:1] / own[1:2]
    scale = 1.0 / jnp.sqrt(f32(n))

    def outgoing(side):
        held_out, ref = ((lb_v, lb_ref), (rb_v, rb_ref))[side]
        return [
            pltpu.make_async_copy(
                held_out.at[pl.ds(start, rows)], ref.at[pl.ds(start, rows)],
                out_sem.at[3 * side + i],
            )
            for i, (start, rows, _) in enumerate(chunks)
        ]

    def extend_side(side):
        _, ops, out, _, arrival = sides[side]
        arrival.wait_recv()
        k = far_kept[side] * norm(totals(2 * side))
        first, second = (k.T, k) if side else (k, k.T)
        weight, streams = stationary(first), streamed(second)
        for i, (start, rows, _) in enumerate(chunks):
            extend(ops, weight, streams, out, scale, start, rows // n, n)
            outgoing(side)[i].start()

    def clear(side):
        out = (lb_v, rb_v)[side]
        out[...] = jnp.zeros_like(out)
        for copy in outgoing(side):
            copy.start()

    pl.when(s == 0)(lambda: clear(0))
    pl.when(s == nseg - 1)(lambda: clear(1))
    pl.when(jnp.logical_and(even, has_up))(lambda: extend_side(1))
    pl.when(has_down)(lambda: extend_side(0))
    pl.when(jnp.logical_and(odd, has_up))(lambda: extend_side(1))

    @pl.when(has_next)
    def _():
        for k in range(ITERS):
            send_v(k).wait_send()

    @pl.when(has_previous)
    def _():
        for k in range(ITERS):
            send_c(k).wait_send()

    send_environments(lambda copy: copy.wait_send())
    on_relay(lambda *way: pl.when(s == way[1])(lambda: from_relay(*way).wait_send()))
    pl.when(has_up)(lambda: kept_up.wait_send())
    pl.when(has_down)(lambda: kept_down.wait_send())
    per_segment(lambda step: per_peer(step, lambda peer, j: sum_copy(step, peer, j).wait_send()))
    for copy in outgoing(0) + outgoing(1) + [state_out]:
        copy.wait()


def write_out(energy_ref, state_ref, left_ref, right_ref, energy_out, state_out, left_out, right_out, *rest):
    refs = (state_ref, left_ref, right_ref, state_out, left_out, right_out)
    loaded, sems = rest[0:3], rest[3]
    energy_out[...] = energy_ref[...]
    copies = []
    for i in range(3):
        rows = refs[i].shape[0]
        step = max(rows // 3, 128)
        for at in range(0, rows, step):
            part = pl.ds(at, min(step, rows - at))
            j = len(copies)
            copies.append(
                (
                    pltpu.make_async_copy(refs[i].at[part], loaded[i].at[part], sems.at[0, j]),
                    pltpu.make_async_copy(loaded[i].at[part], refs[3 + i].at[part], sems.at[1, j]),
                )
            )
    for load, _ in copies:
        load.start()
    for load, store in copies:
        load.wait()
        store.start()
    for _, store in copies:
        store.wait()


def shards(nseg, nblk, two_site, diag_left, diag_right, hop_left, hop_right, sector_sizes, ranks):
    n = two_site.shape[2]
    ndiag, nhop = diag_left.shape[2], hop_left.shape[2]
    nch = ndiag + nhop
    smem = pl.BlockSpec(memory_space=pltpu.SMEM)
    vmem = pl.BlockSpec(memory_space=pltpu.VMEM)
    hbm = pl.BlockSpec(memory_space=pltpu.HBM)
    dma = pltpu.SemaphoreType.DMA
    state, left, right, energy = pl.pallas_call(
        functools.partial(kernel, nseg, nblk, ndiag, nhop, n),
        out_shape=(
            jax.ShapeDtypeStruct((n, n), f32),
            jax.ShapeDtypeStruct((nch * n, n), f32),
            jax.ShapeDtypeStruct((nch * n, n), f32),
            jax.ShapeDtypeStruct((1, 1), f32),
        ),
        in_specs=[smem, smem] + [hbm] * 5,
        out_specs=(hbm, hbm, hbm, vmem),
        scratch_shapes=[
            pltpu.VMEM((nch * n, n), f32),
            pltpu.VMEM((nch * n, n), f32),
            pltpu.VMEM((nch * n, n), f32),
            pltpu.VMEM((nch * n, n), f32),
            pltpu.VMEM((n, n), f32),
            pltpu.VMEM((nch * n, n), f32),
            pltpu.VMEM((nch * n, n), f32),
            pltpu.VMEM((nch * n, 2 * n), bf16),
            pltpu.VMEM((nhop * n, 2 * n), bf16),
            pltpu.VMEM((nhop * n, 2 * n), bf16),
            pltpu.VMEM((nch * n, 2 * n), bf16),
            pltpu.VMEM((nch * n, 2 * n), bf16),
            pltpu.VMEM((nch * n, 2 * n), bf16),
            pltpu.VMEM((2 * n, nch * n), bf16),
            pltpu.VMEM((ITERS + 1, n, n), f32),
            pltpu.VMEM((ITERS + 1, n, n), f32),
            pltpu.VMEM((ITERS, n, n), f32),
            pltpu.VMEM((ITERS, n, n), f32),
            pltpu.VMEM((n, n), f32),
            pltpu.VMEM((2, n, n), f32),
            pltpu.VMEM((3, nblk, 8, n), f32),
            dma((5,)),
            dma((ITERS,)),
            dma((ITERS,)),
            dma((ITERS,)),
            dma((ITERS,)),
            dma((6,)),
            dma((6,)),
            dma((2,)),
            dma((2,)),
            dma((3, nblk)),
            dma((3, nblk)),
            dma((7,)),
            pltpu.VMEM((nhop * n - nhop // 2 * n, n), f32),
            dma((2,)),
            dma((1,)),
        ],
        compiler_params=pltpu.CompilerParams(
            collective_id=0, has_side_effects=True, vmem_limit_bytes=57 * 1024 * 1024
        ),
        name="solve",
    )(
        sector_sizes, ranks,
        two_site.reshape(n, n),
        diag_left.reshape(ndiag * n, n),
        diag_right.reshape(ndiag * n, n),
        hop_left.reshape(nhop * n, n),
        hop_right.reshape(nhop * n, n),
    )
    energy, state, left, right = pl.pallas_call(
        write_out,
        out_shape=tuple(jax.ShapeDtypeStruct(x.shape, f32) for x in (energy, state, left, right)),
        in_specs=[vmem] + [hbm] * 3,
        out_specs=(vmem,) + (hbm,) * 3,
        scratch_shapes=[pltpu.VMEM(x.shape, f32) for x in (state, left, right)] + [dma((2, 8))],
        compiler_params=pltpu.CompilerParams(vmem_limit_bytes=57 * 1024 * 1024),
        name="write_out",
    )(energy, state, left, right)
    return (
        state.reshape(1, 1, n, n),
        left.reshape(1, 1, nch, n, n),
        right.reshape(1, 1, nch, n, n),
        energy.reshape(1),
    )


def solution(mesh):
    nseg, nblk = mesh.shape["seg"], mesh.shape["blk"]
    return jax.shard_map(
        functools.partial(shards, nseg, nblk),
        mesh=mesh,
        in_specs=(
            P("seg", "blk", None, None),
            P("seg", "blk", None, None, None),
            P("seg", "blk", None, None, None),
            P("seg", "blk", None, None, None),
            P("seg", "blk", None, None, None),
            P("seg", "blk"),
            P("seg", "blk"),
        ),
        out_specs=(
            P("seg", "blk", None, None),
            P("seg", "blk", None, None, None),
            P("seg", "blk", None, None, None),
            P("seg"),
        ),
        check_vma=False,
    )
```

```python
import functools

import jax
import jax.numpy as jnp
from jax import lax
from jax.experimental import pallas as pl
from jax.experimental.pallas import tpu as pltpu
from jax.sharding import PartitionSpec as P

ITERS = 4
BATCH = 4
MESH = pl.DeviceIdType.MESH
f32 = jnp.float32
bf16 = jnp.bfloat16
spectral_shift = 20.0


def split(x):
    hi = x.astype(bf16)
    lo = (x - hi.astype(f32)).astype(bf16)
    return hi, lo


def stationary(x):
    hi, lo = split(x)
    top = jnp.concatenate([hi, lo], 1)
    low = jnp.concatenate([hi, jnp.zeros_like(hi)], 1)
    return jnp.concatenate([top, low], 0)


def streamed(x):
    hi, lo = split(x)
    top = jnp.concatenate([hi, hi], 1)
    low = jnp.concatenate([lo, jnp.zeros_like(lo)], 1)
    return jnp.concatenate([top, low], 0)


def dot(a, b):
    return jnp.dot(a, b, preferred_element_type=f32)


def prepare(source, rows, target, at, transpose, n):
    x = source[pl.ds(rows, n), :]
    hi, lo = split(x.T if transpose else x)
    target[pl.ds(at, n), 0:n] = hi
    target[pl.ds(at, n), n : 2 * n] = lo


def first_stage(ops, start, count, weight, held, column, n):
    got = dot(ops[start : start + count * n, :], weight)
    got = got[:, 0:n] + got[:, n : 2 * n]
    hi, lo = split(got)
    for c in range(count):
        lanes = column + c * n
        held[0:n, lanes : lanes + n] = hi[c * n : (c + 1) * n]
        held[n : 2 * n, lanes : lanes + n] = lo[c * n : (c + 1) * n]


def second_stage(held, column, count, ops, start, n):
    got = dot(held[:, column : column + count * n], ops[start : start + count * n, :])
    return (got[0:n, 0:n] + got[0:n, n : 2 * n]) + (got[n : 2 * n, 0:n] + got[n : 2 * n, n : 2 * n])


def both_stages(left, right, start, count, weight, held, n):
    total, waiting = None, None
    for c in list(range(0, count, BATCH)) + [None]:
        if c is not None:
            size = min(BATCH, count - c)
            first_stage(left, start + c * n, size, weight, held, start + c * n, n)
        if waiting is not None:
            at, some = waiting
            term = second_stage(held, at, some, right, at, n)
            total = term if total is None else total + term
        waiting = None if c is None else (start + c * n, size)
    return total


def extend(ops, weight, rows, out, scale, start, count, n):
    got = dot(ops[start : start + count * n, :], weight)
    got = got[:, 0:n] + got[:, n : 2 * n]
    hi, lo = split(got)
    tops = [hi[c * n : (c + 1) * n] for c in range(count)]
    lows = [lo[c * n : (c + 1) * n] for c in range(count)]
    wide = jnp.concatenate([jnp.concatenate(tops, 1), jnp.concatenate(lows, 1)], 0)
    done = dot(rows, wide)
    done = (done[0:n] + done[n:]) * scale
    for c in range(count):
        out[start + c * n : start + (c + 1) * n, :] = done[:, c * n : (c + 1) * n]


def kernel(
    nseg, nblk, ndiag, nhop, n,
    size_ref, rank_ref, two_ref, dl_ref, dr_ref, hl_ref, hr_ref,
    state_ref, lb_ref, rb_ref, energy_ref,
    xl, yr, far_x, far_y, state_v, lb_v, rb_v, a2, at2, b2, bt2, fx2, fy2, held,
    v_buf, c_buf, rv, rc, kept, far_kept, sums,
    load_sem, v_send, v_recv, c_send, c_recv, x_send, x_recv, k_send, k_recv, s_send, s_recv, out_sem, relay, r_send, r_recv,
):
    s = lax.axis_index("seg")
    q = lax.axis_index("blk")
    nch = ndiag + nhop
    small = ndiag * n

    loads = [
        pltpu.make_async_copy(src, dst, load_sem.at[i])
        for i, (src, dst) in enumerate(
            (
                (two_ref, c_buf.at[ITERS]),
                (hl_ref, xl.at[pl.ds(small, nhop * n)]),
                (hr_ref, yr.at[pl.ds(small, nhop * n)]),
                (dl_ref, xl.at[pl.ds(0, small)]),
                (dr_ref, yr.at[pl.ds(0, small)]),
            )
        )
    ]
    for load in loads:
        load.start()

    def per_segment(action):
        action(0)
        pl.when(s < nseg - 1)(lambda: action(1))
        pl.when(s > 0)(lambda: action(-1))

    def per_peer(step, action):
        def body(j, carry):
            action(lax.rem(q + j, nblk), j)
            return carry

        lax.fori_loop(1 if step == 0 else 0, nblk, body, 0, unroll=nblk <= 8)

    barrier = pltpu.get_barrier_semaphore()

    def greet(step):
        per_peer(
            step,
            lambda peer, j: pl.semaphore_signal(
                barrier, inc=1, device_id={"seg": s + step, "blk": peer}, device_id_type=MESH
            ),
        )

    per_segment(greet)

    below, above = nseg // 2 - 1, nseg // 2
    relays = ((below, nseg - 1, above), (above, 0, below))

    def on_relay(action):
        for origin, via, target in relays:
            action(origin, via, target)

    def greet_relay(origin, via, target):
        for first, second in ((origin, via), (via, origin), (via, target), (target, via)):
            @pl.when(s == first)
            def _(second=second):
                pl.semaphore_signal(
                    barrier, inc=1, device_id={"seg": second, "blk": q}, device_id_type=MESH
                )

    on_relay(greet_relay)

    @pl.when(q == 0)
    def _():
        rv[...] = jnp.zeros_like(rv)

    @pl.when(q == nblk - 1)
    def _():
        rc[...] = jnp.zeros_like(rc)

    size = size_ref[0, 0]
    count = jnp.minimum(rank_ref[0, 0], size)
    row_at = lax.broadcasted_iota(jnp.int32, (n, n), 0)
    col_at = lax.broadcasted_iota(jnp.int32, (n, n), 1)
    live = jnp.where(jnp.maximum(row_at, col_at) < size, 1.0, 0.0).astype(f32)
    col_live = jnp.where(col_at < count, 1.0, 0.0).astype(f32)

    loads[0].wait()
    v_buf[0] = live * c_buf[ITERS]

    groups = 1 + jnp.minimum(s, 1) + jnp.minimum(nseg - 1 - s, 1)
    others = 0
    for place in (0, below, above, nseg - 1):
        others = others + 2 * (1 - jnp.minimum(jnp.maximum(s - place, place - s), 1))
    pl.semaphore_wait(barrier, groups * nblk - 1 + others)

    def remote(src, dst, send, recv, where):
        return pltpu.make_async_remote_copy(
            src_ref=src, dst_ref=dst, send_sem=send, recv_sem=recv,
            device_id=where, device_id_type=MESH,
        )

    def send_v(k):
        return remote(v_buf.at[k], rv.at[k], v_send.at[k], v_recv.at[k], {"seg": s, "blk": q + 1})

    def send_c(k):
        return remote(c_buf.at[k], rc.at[k], c_send.at[k], c_recv.at[k], {"seg": s, "blk": q - 1})

    up, down = {"seg": s + 1, "blk": q}, {"seg": s - 1, "blk": q}
    half = nhop // 2 * n
    chunks = [(small, half, 1), (small + half, nhop * n - half, 1), (0, small, 0)]

    def environment(refs, far, first, where):
        return [
            remote(
                refs[hop].at[pl.ds(start - small * hop, rows)],
                far.at[pl.ds(start, rows)],
                x_send.at[first + i], x_recv.at[first + i], where,
            )
            for i, (start, rows, hop) in enumerate(chunks)
        ]

    to_up = environment((dl_ref, hl_ref), far_x, 0, up)
    to_down = environment((dr_ref, hr_ref), far_y, 3, down)
    kept_up = remote(kept, far_kept.at[0], k_send.at[0], k_recv.at[0], up)
    kept_down = remote(kept, far_kept.at[1], k_send.at[1], k_recv.at[1], down)

    has_next, has_previous = q < nblk - 1, q > 0
    has_up, has_down = s < nseg - 1, s > 0

    pl.when(has_next)(lambda: send_v(0).start())

    def to_relay(origin, via, target):
        start, rows, _ = chunks[1]
        source = hl_ref if origin < target else hr_ref
        return remote(
            source.at[pl.ds(start - small, rows)], relay, r_send.at[0], r_recv.at[0],
            {"seg": via, "blk": q},
        )

    def from_relay(origin, via, target):
        start, rows, _ = chunks[1]
        far, i = (far_x, 1) if origin < target else (far_y, 4)
        return remote(
            relay, far.at[pl.ds(start, rows)], r_send.at[1], x_recv.at[i],
            {"seg": target, "blk": q},
        )

    def send_environments(action):
        on_relay(lambda *way: pl.when(s == way[0])(lambda: action(to_relay(*way))))
        for copies, some, middle in ((to_up, has_up, below), (to_down, has_down, above)):
            pl.when(some)(lambda: action(copies[0]))
            pl.when(jnp.logical_and(some, s != middle))(lambda: action(copies[1]))
            pl.when(some)(lambda: action(copies[2]))

    def pass_on(*way):
        @pl.when(s == way[1])
        def _():
            to_relay(*way).wait_recv()
            from_relay(*way).start()

    send_environments(lambda copy: copy.start())

    loads[1].wait()
    loads[2].wait()
    for h in range(nhop):
        at = small + h * n
        prepare(xl, at, at2, h * n, True, n)
        prepare(yr, at, b2, h * n, False, n)

    def carried(k):
        c_buf[k] = both_stages(at2, b2, 0, nhop, stationary(v_buf[k]), held, n)
        pl.when(has_previous)(lambda: send_c(k).start())

    def finish(k):
        own = both_stages(a2, bt2, 0, ndiag, stationary(v_buf[k]), held, n)
        pl.when(has_previous)(lambda: send_v(k).wait_recv())
        own = own + both_stages(a2, bt2, small, nhop, stationary(rv[k]), held, n)
        pl.when(has_next)(lambda: send_c(k).wait_recv())
        applied = live * (own + rc[k])
        vector = spectral_shift * v_buf[k] - applied
        v_buf[k + 1] = vector
        return applied, vector

    carried(0)
    loads[3].wait()
    loads[4].wait()
    for c in range(nch):
        prepare(xl, c * n, a2, c * n, False, n)
        prepare(yr, c * n, bt2, c * n, True, n)
    finish(0)
    pl.when(has_next)(lambda: send_v(1).start())

    sides = ((far_x, fx2, lb_v, to_up, kept_up), (far_y, fy2, rb_v, to_down, kept_down))
    even = lax.rem(s, 2) == 0
    odd = jnp.logical_not(even)

    def prepare_side(side):
        far, ops, _, copies, _ = sides[side]
        for copy in copies:
            copy.wait_recv()
        for c in range(nch):
            prepare(far, c * n, ops, c * n, side == 1, n)

    def middle(k, carry):
        carried(k)
        finish(k)
        pl.when(has_next)(lambda: send_v(k + 1).start())
        pl.when(k == 1)(lambda: on_relay(pass_on))
        return carry

    lax.fori_loop(1, ITERS - 1, middle, 0)
    carried(ITERS - 1)
    pl.when(jnp.logical_and(even, has_up))(lambda: prepare_side(1))
    pl.when(jnp.logical_and(odd, has_down))(lambda: prepare_side(0))
    applied, vector = finish(ITERS - 1)
    last = v_buf[ITERS - 1]
    kept[...] = vector * col_live
    pl.when(has_up)(lambda: kept_up.start())
    pl.when(has_down)(lambda: kept_down.start())

    def rowsum(x):
        return jnp.sum(x, 0, keepdims=True)

    row8 = lax.broadcasted_iota(jnp.int32, (8, n), 0)
    tile = jnp.where(row8 == 0, rowsum(last * applied), 0.0)
    tile = jnp.where(row8 == 1, rowsum(last * last), tile)
    tile = jnp.where(row8 == 2, rowsum(vector * vector), tile)
    tile = jnp.where(row8 == 3, size.astype(f32) * (1.0 / n), tile)
    sums[1, q] = tile

    def sum_copy(step, peer, j):
        group = 1 - step
        return remote(
            sums.at[1, q], sums.at[group, q], s_send.at[group, j], s_recv.at[group, q],
            {"seg": s + step, "blk": peer},
        )

    def sum_arrival(group, peer):
        return remote(
            sums.at[1, q], sums.at[group, peer], s_send.at[group, 0], s_recv.at[group, peer],
            {"seg": s, "blk": peer},
        )

    per_segment(lambda step: per_peer(step, lambda peer, j: sum_copy(step, peer, j).start()))

    pl.when(jnp.logical_and(even, has_down))(lambda: prepare_side(0))
    pl.when(jnp.logical_and(odd, has_up))(lambda: prepare_side(1))

    def totals(group):
        step = 0 if group == 1 else 1
        per_peer(step, lambda peer, j: sum_arrival(group, peer).wait_recv())
        total = sums[group, 0]
        for j in range(1, nblk):
            total = total + sums[group, j]
        return jnp.sum(total, 1, keepdims=True)

    def norm(total):
        return jnp.sqrt(total[3:4] * n / total[2:3])

    own = totals(1)
    state_v[...] = vector * norm(own)
    state_out = pltpu.make_async_copy(state_v, state_ref, out_sem.at[6])
    state_out.start()
    energy_ref[...] = own[0:1] / own[1:2]
    scale = 1.0 / jnp.sqrt(f32(n))

    def outgoing(side):
        held_out, ref = ((lb_v, lb_ref), (rb_v, rb_ref))[side]
        return [
            pltpu.make_async_copy(
                held_out.at[pl.ds(start, rows)], ref.at[pl.ds(start, rows)],
                out_sem.at[3 * side + i],
            )
            for i, (start, rows, _) in enumerate(chunks)
        ]

    def extend_side(side):
        _, ops, out, _, arrival = sides[side]
        arrival.wait_recv()
        k = far_kept[side] * norm(totals(2 * side))
        first, second = (k.T, k) if side else (k, k.T)
        weight, streams = stationary(first), streamed(second)
        for i, (start, rows, _) in enumerate(chunks):
            extend(ops, weight, streams, out, scale, start, rows // n, n)
            outgoing(side)[i].start()

    def clear(side):
        out = (lb_v, rb_v)[side]
        out[...] = jnp.zeros_like(out)
        for copy in outgoing(side):
            copy.start()

    pl.when(s == 0)(lambda: clear(0))
    pl.when(s == nseg - 1)(lambda: clear(1))
    pl.when(jnp.logical_and(even, has_up))(lambda: extend_side(1))
    pl.when(has_down)(lambda: extend_side(0))
    pl.when(jnp.logical_and(odd, has_up))(lambda: extend_side(1))

    @pl.when(has_next)
    def _():
        for k in range(ITERS):
            send_v(k).wait_send()

    @pl.when(has_previous)
    def _():
        for k in range(ITERS):
            send_c(k).wait_send()

    send_environments(lambda copy: copy.wait_send())
    on_relay(lambda *way: pl.when(s == way[1])(lambda: from_relay(*way).wait_send()))
    pl.when(has_up)(lambda: kept_up.wait_send())
    pl.when(has_down)(lambda: kept_down.wait_send())
    per_segment(lambda step: per_peer(step, lambda peer, j: sum_copy(step, peer, j).wait_send()))
    for copy in outgoing(0) + outgoing(1) + [state_out]:
        copy.wait()


def write_out(*refs):
    loaded, sems = refs[8:12], refs[12]
    copies = []
    for i in range(4):
        rows = refs[i].shape[0]
        step = max(rows // 3, 128)
        for at in range(0, rows, step):
            size = min(step, rows - at)
            j = len(copies)
            part = (lambda ref: ref) if size == rows else (lambda ref: ref.at[pl.ds(at, size)])
            source, middle, target = part(refs[i]), part(loaded[i]), part(refs[4 + i])
            copies.append(
                (
                    pltpu.make_async_copy(source, middle, sems.at[0, j]),
                    pltpu.make_async_copy(middle, target, sems.at[1, j]),
                )
            )
    for load, _ in copies:
        load.start()
    for load, store in copies:
        load.wait()
        store.start()
    for _, store in copies:
        store.wait()


def shards(nseg, nblk, two_site, diag_left, diag_right, hop_left, hop_right, sector_sizes, ranks):
    n = two_site.shape[2]
    ndiag, nhop = diag_left.shape[2], hop_left.shape[2]
    nch = ndiag + nhop
    smem = pl.BlockSpec(memory_space=pltpu.SMEM)
    vmem = pl.BlockSpec(memory_space=pltpu.VMEM)
    hbm = pl.BlockSpec(memory_space=pltpu.HBM)
    dma = pltpu.SemaphoreType.DMA
    state, left, right, energy = pl.pallas_call(
        functools.partial(kernel, nseg, nblk, ndiag, nhop, n),
        out_shape=(
            jax.ShapeDtypeStruct((n, n), f32),
            jax.ShapeDtypeStruct((nch * n, n), f32),
            jax.ShapeDtypeStruct((nch * n, n), f32),
            jax.ShapeDtypeStruct((1, 1), f32),
        ),
        in_specs=[smem, smem] + [hbm] * 5,
        out_specs=(hbm, hbm, hbm, vmem),
        scratch_shapes=[
            pltpu.VMEM((nch * n, n), f32),
            pltpu.VMEM((nch * n, n), f32),
            pltpu.VMEM((nch * n, n), f32),
            pltpu.VMEM((nch * n, n), f32),
            pltpu.VMEM((n, n), f32),
            pltpu.VMEM((nch * n, n), f32),
            pltpu.VMEM((nch * n, n), f32),
            pltpu.VMEM((nch * n, 2 * n), bf16),
            pltpu.VMEM((nhop * n, 2 * n), bf16),
            pltpu.VMEM((nhop * n, 2 * n), bf16),
            pltpu.VMEM((nch * n, 2 * n), bf16),
            pltpu.VMEM((nch * n, 2 * n), bf16),
            pltpu.VMEM((nch * n, 2 * n), bf16),
            pltpu.VMEM((2 * n, nch * n), bf16),
            pltpu.VMEM((ITERS + 1, n, n), f32),
            pltpu.VMEM((ITERS + 1, n, n), f32),
            pltpu.VMEM((ITERS, n, n), f32),
            pltpu.VMEM((ITERS, n, n), f32),
            pltpu.VMEM((n, n), f32),
            pltpu.VMEM((2, n, n), f32),
            pltpu.VMEM((3, nblk, 8, n), f32),
            dma((5,)),
            dma((ITERS,)),
            dma((ITERS,)),
            dma((ITERS,)),
            dma((ITERS,)),
            dma((6,)),
            dma((6,)),
            dma((2,)),
            dma((2,)),
            dma((3, nblk)),
            dma((3, nblk)),
            dma((7,)),
            pltpu.VMEM((nhop * n - nhop // 2 * n, n), f32),
            dma((2,)),
            dma((1,)),
        ],
        compiler_params=pltpu.CompilerParams(
            collective_id=0, has_side_effects=True, vmem_limit_bytes=57 * 1024 * 1024
        ),
        name="solve",
    )(
        sector_sizes, ranks,
        two_site.reshape(n, n),
        diag_left.reshape(ndiag * n, n),
        diag_right.reshape(ndiag * n, n),
        hop_left.reshape(nhop * n, n),
        hop_right.reshape(nhop * n, n),
    )
    energy, state, left, right = pl.pallas_call(
        write_out,
        out_shape=tuple(jax.ShapeDtypeStruct(x.shape, f32) for x in (energy, state, left, right)),
        in_specs=[hbm] * 4,
        out_specs=(hbm,) * 4,
        scratch_shapes=[pltpu.VMEM(x.shape, f32) for x in (energy, state, left, right)]
        + [dma((2, 8))],
        compiler_params=pltpu.CompilerParams(vmem_limit_bytes=57 * 1024 * 1024),
        name="write_out",
    )(energy, state, left, right)
    return (
        state.reshape(1, 1, n, n),
        left.reshape(1, 1, nch, n, n),
        right.reshape(1, 1, nch, n, n),
        energy.reshape(1),
    )


def solution(mesh):
    nseg, nblk = mesh.shape["seg"], mesh.shape["blk"]
    return jax.shard_map(
        functools.partial(shards, nseg, nblk),
        mesh=mesh,
        in_specs=(
            P("seg", "blk", None, None),
            P("seg", "blk", None, None, None),
            P("seg", "blk", None, None, None),
            P("seg", "blk", None, None, None),
            P("seg", "blk", None, None, None),
            P("seg", "blk"),
            P("seg", "blk"),
        ),
        out_specs=(
            P("seg", "blk", None, None),
            P("seg", "blk", None, None, None),
            P("seg", "blk", None, None, None),
            P("seg"),
        ),
        check_vma=False,
    )
```

```python
import functools

import jax
import jax.numpy as jnp
from jax import lax
from jax.experimental import pallas as pl
from jax.experimental.pallas import tpu as pltpu
from jax.sharding import PartitionSpec as P

ITERS = 4
BATCH = 4
MESH = pl.DeviceIdType.MESH
f32 = jnp.float32
bf16 = jnp.bfloat16
spectral_shift = 20.0


def split(x):
    hi = x.astype(bf16)
    lo = (x - hi.astype(f32)).astype(bf16)
    return hi, lo


def stationary(x):
    hi, lo = split(x)
    top = jnp.concatenate([hi, lo], 1)
    low = jnp.concatenate([hi, jnp.zeros_like(hi)], 1)
    return jnp.concatenate([top, low], 0)


def streamed(x):
    hi, lo = split(x)
    top = jnp.concatenate([hi, hi], 1)
    low = jnp.concatenate([lo, jnp.zeros_like(lo)], 1)
    return jnp.concatenate([top, low], 0)


def dot(a, b):
    return jnp.dot(a, b, preferred_element_type=f32)


def prepare(source, rows, target, at, transpose, n):
    x = source[pl.ds(rows, n), :]
    hi, lo = split(x.T if transpose else x)
    target[pl.ds(at, n), 0:n] = hi
    target[pl.ds(at, n), n : 2 * n] = lo


def first_stage(ops, start, count, weight, held, column, n):
    got = dot(ops[start : start + count * n, :], weight)
    got = got[:, 0:n] + got[:, n : 2 * n]
    hi, lo = split(got)
    for c in range(count):
        lanes = column + c * n
        held[0:n, lanes : lanes + n] = hi[c * n : (c + 1) * n]
        held[n : 2 * n, lanes : lanes + n] = lo[c * n : (c + 1) * n]


def second_stage(held, column, count, ops, start, n):
    got = dot(held[:, column : column + count * n], ops[start : start + count * n, :])
    return (got[0:n, 0:n] + got[0:n, n : 2 * n]) + (got[n : 2 * n, 0:n] + got[n : 2 * n, n : 2 * n])


def both_stages(left, right, start, count, weight, held, n):
    total, waiting = None, None
    for c in list(range(0, count, BATCH)) + [None]:
        if c is not None:
            size = min(BATCH, count - c)
            first_stage(left, start + c * n, size, weight, held, start + c * n, n)
        if waiting is not None:
            at, some = waiting
            term = second_stage(held, at, some, right, at, n)
            total = term if total is None else total + term
        waiting = None if c is None else (start + c * n, size)
    return total


def extend(ops, weight, rows, out, scale, start, count, n):
    got = dot(ops[start : start + count * n, :], weight)
    got = got[:, 0:n] + got[:, n : 2 * n]
    hi, lo = split(got)
    tops = [hi[c * n : (c + 1) * n] for c in range(count)]
    lows = [lo[c * n : (c + 1) * n] for c in range(count)]
    wide = jnp.concatenate([jnp.concatenate(tops, 1), jnp.concatenate(lows, 1)], 0)
    done = dot(rows, wide)
    done = (done[0:n] + done[n:]) * scale
    for c in range(count):
        out[start + c * n : start + (c + 1) * n, :] = done[:, c * n : (c + 1) * n]


def kernel(
    nseg, nblk, ndiag, nhop, n,
    size_ref, rank_ref, two_ref, dl_ref, dr_ref, hl_ref, hr_ref,
    state_ref, lb_ref, rb_ref, energy_ref,
    xl, yr, far_x, far_y, state_v, lb_v, rb_v, a2, at2, b2, bt2, fx2, fy2, held,
    v_buf, c_buf, rv, rc, kept, far_kept, sums,
    load_sem, v_send, v_recv, c_send, c_recv, x_send, x_recv, k_send, k_recv, s_send, s_recv, out_sem, relay, r_send, r_recv,
):
    s = lax.axis_index("seg")
    q = lax.axis_index("blk")
    nch = ndiag + nhop
    small = ndiag * n

    loads = [
        pltpu.make_async_copy(src, dst, load_sem.at[i])
        for i, (src, dst) in enumerate(
            (
                (two_ref, c_buf.at[ITERS]),
                (hl_ref, xl.at[pl.ds(small, nhop * n)]),
                (hr_ref, yr.at[pl.ds(small, nhop * n)]),
                (dl_ref, xl.at[pl.ds(0, small)]),
                (dr_ref, yr.at[pl.ds(0, small)]),
            )
        )
    ]
    for load in loads:
        load.start()

    def per_segment(action):
        action(0)
        pl.when(s < nseg - 1)(lambda: action(1))
        pl.when(s > 0)(lambda: action(-1))

    def per_peer(step, action):
        def body(j, carry):
            action(lax.rem(q + j, nblk), j)
            return carry

        lax.fori_loop(1 if step == 0 else 0, nblk, body, 0, unroll=nblk <= 8)

    barrier = pltpu.get_barrier_semaphore()

    def greet(step):
        per_peer(
            step,
            lambda peer, j: pl.semaphore_signal(
                barrier, inc=1, device_id={"seg": s + step, "blk": peer}, device_id_type=MESH
            ),
        )

    per_segment(greet)

    below, above = nseg // 2 - 1, nseg // 2
    relays = ((below, nseg - 1, above), (above, 0, below))

    def on_relay(action):
        for origin, via, target in relays:
            action(origin, via, target)

    def greet_relay(origin, via, target):
        for first, second in ((origin, via), (via, origin), (via, target), (target, via)):
            @pl.when(s == first)
            def _(second=second):
                pl.semaphore_signal(
                    barrier, inc=1, device_id={"seg": second, "blk": q}, device_id_type=MESH
                )

    on_relay(greet_relay)

    @pl.when(q == 0)
    def _():
        rv[...] = jnp.zeros_like(rv)

    @pl.when(q == nblk - 1)
    def _():
        rc[...] = jnp.zeros_like(rc)

    size = size_ref[0, 0]
    count = jnp.minimum(rank_ref[0, 0], size)
    row_at = lax.broadcasted_iota(jnp.int32, (n, n), 0)
    col_at = lax.broadcasted_iota(jnp.int32, (n, n), 1)
    live = jnp.where(jnp.maximum(row_at, col_at) < size, 1.0, 0.0).astype(f32)
    col_live = jnp.where(col_at < count, 1.0, 0.0).astype(f32)

    loads[0].wait()
    v_buf[0] = live * c_buf[ITERS]

    groups = 1 + jnp.minimum(s, 1) + jnp.minimum(nseg - 1 - s, 1)
    others = 0
    for place in (0, below, above, nseg - 1):
        others = others + 2 * (1 - jnp.minimum(jnp.maximum(s - place, place - s), 1))
    pl.semaphore_wait(barrier, groups * nblk - 1 + others)

    def remote(src, dst, send, recv, where):
        return pltpu.make_async_remote_copy(
            src_ref=src, dst_ref=dst, send_sem=send, recv_sem=recv,
            device_id=where, device_id_type=MESH,
        )

    def send_v(k):
        return remote(v_buf.at[k], rv.at[k], v_send.at[k], v_recv.at[k], {"seg": s, "blk": q + 1})

    def send_c(k):
        return remote(c_buf.at[k], rc.at[k], c_send.at[k], c_recv.at[k], {"seg": s, "blk": q - 1})

    up, down = {"seg": s + 1, "blk": q}, {"seg": s - 1, "blk": q}
    half = (nhop // 2 - 1) * n
    chunks = [(small, half, 1), (small + half, nhop * n - half, 1), (0, small, 0)]

    def environment(refs, far, first, where):
        return [
            remote(
                refs[hop].at[pl.ds(start - small * hop, rows)],
                far.at[pl.ds(start, rows)],
                x_send.at[first + i], x_recv.at[first + i], where,
            )
            for i, (start, rows, hop) in enumerate(chunks)
        ]

    to_up = environment((dl_ref, hl_ref), far_x, 0, up)
    to_down = environment((dr_ref, hr_ref), far_y, 3, down)
    kept_up = remote(kept, far_kept.at[0], k_send.at[0], k_recv.at[0], up)
    kept_down = remote(kept, far_kept.at[1], k_send.at[1], k_recv.at[1], down)

    has_next, has_previous = q < nblk - 1, q > 0
    has_up, has_down = s < nseg - 1, s > 0

    pl.when(has_next)(lambda: send_v(0).start())

    def to_relay(origin, via, target):
        start, rows, _ = chunks[1]
        source = hl_ref if origin < target else hr_ref
        return remote(
            source.at[pl.ds(start - small, rows)], relay, r_send.at[0], r_recv.at[0],
            {"seg": via, "blk": q},
        )

    def from_relay(origin, via, target):
        start, rows, _ = chunks[1]
        far, i = (far_x, 1) if origin < target else (far_y, 4)
        return remote(
            relay, far.at[pl.ds(start, rows)], r_send.at[1], x_recv.at[i],
            {"seg": target, "blk": q},
        )

    def send_environments(action):
        on_relay(lambda *way: pl.when(s == way[0])(lambda: action(to_relay(*way))))
        for copies, some, middle in ((to_up, has_up, below), (to_down, has_down, above)):
            pl.when(some)(lambda: action(copies[0]))
            pl.when(jnp.logical_and(some, s != middle))(lambda: action(copies[1]))
            pl.when(some)(lambda: action(copies[2]))

    def pass_on(*way):
        @pl.when(s == way[1])
        def _():
            to_relay(*way).wait_recv()
            from_relay(*way).start()

    send_environments(lambda copy: copy.start())

    loads[1].wait()
    loads[2].wait()
    for h in range(nhop):
        at = small + h * n
        prepare(xl, at, at2, h * n, True, n)
        prepare(yr, at, b2, h * n, False, n)

    def carried(k):
        c_buf[k] = both_stages(at2, b2, 0, nhop, stationary(v_buf[k]), held, n)
        pl.when(has_previous)(lambda: send_c(k).start())

    def finish(k):
        own = both_stages(a2, bt2, 0, ndiag, stationary(v_buf[k]), held, n)
        pl.when(has_previous)(lambda: send_v(k).wait_recv())
        own = own + both_stages(a2, bt2, small, nhop, stationary(rv[k]), held, n)
        pl.when(has_next)(lambda: send_c(k).wait_recv())
        applied = live * (own + rc[k])
        vector = spectral_shift * v_buf[k] - applied
        v_buf[k + 1] = vector
        return applied, vector

    carried(0)
    loads[3].wait()
    loads[4].wait()
    for c in range(nch):
        prepare(xl, c * n, a2, c * n, False, n)
        prepare(yr, c * n, bt2, c * n, True, n)
    finish(0)
    pl.when(has_next)(lambda: send_v(1).start())

    sides = ((far_x, fx2, lb_v, to_up, kept_up), (far_y, fy2, rb_v, to_down, kept_down))
    even = lax.rem(s, 2) == 0
    odd = jnp.logical_not(even)

    def prepare_chunk(side, i):
        far, ops, _, copies, _ = sides[side]
        start, rows, _ = chunks[i]
        copies[i].wait_recv()
        for at in range(start, start + rows, n):
            prepare(far, at, ops, at, side == 1, n)

    def prepare_side(side):
        for i in range(len(chunks)):
            prepare_chunk(side, i)

    def middle(k, carry):
        carried(k)
        finish(k)
        pl.when(has_next)(lambda: send_v(k + 1).start())
        pl.when(k == 1)(lambda: on_relay(pass_on))
        return carry

    lax.fori_loop(1, ITERS - 1, middle, 0)
    carried(ITERS - 1)
    pl.when(jnp.logical_and(even, has_up))(lambda: prepare_side(1))
    pl.when(jnp.logical_and(odd, has_down))(lambda: prepare_side(0))
    applied, vector = finish(ITERS - 1)
    last = v_buf[ITERS - 1]
    kept[...] = vector * col_live
    pl.when(has_up)(lambda: kept_up.start())
    pl.when(has_down)(lambda: kept_down.start())

    def rowsum(x):
        return jnp.sum(x, 0, keepdims=True)

    row8 = lax.broadcasted_iota(jnp.int32, (8, n), 0)
    tile = jnp.where(row8 == 0, rowsum(last * applied), 0.0)
    tile = jnp.where(row8 == 1, rowsum(last * last), tile)
    tile = jnp.where(row8 == 2, rowsum(vector * vector), tile)
    tile = jnp.where(row8 == 3, size.astype(f32) * (1.0 / n), tile)
    sums[1, q] = tile

    def sum_copy(step, peer, j):
        group = 1 - step
        return remote(
            sums.at[1, q], sums.at[group, q], s_send.at[group, j], s_recv.at[group, q],
            {"seg": s + step, "blk": peer},
        )

    def sum_arrival(group, peer):
        return remote(
            sums.at[1, q], sums.at[group, peer], s_send.at[group, 0], s_recv.at[group, peer],
            {"seg": s, "blk": peer},
        )

    per_segment(lambda step: per_peer(step, lambda peer, j: sum_copy(step, peer, j).start()))

    pl.when(jnp.logical_and(even, has_down))(lambda: prepare_chunk(0, 0))
    pl.when(jnp.logical_and(odd, has_up))(lambda: prepare_chunk(1, 0))

    def totals(group):
        step = 0 if group == 1 else 1
        per_peer(step, lambda peer, j: sum_arrival(group, peer).wait_recv())
        total = sums[group, 0]
        for j in range(1, nblk):
            total = total + sums[group, j]
        return jnp.sum(total, 1, keepdims=True)

    def norm(total):
        return jnp.sqrt(total[3:4] * n / total[2:3])

    own = totals(1)
    state_v[...] = vector * norm(own)
    state_out = pltpu.make_async_copy(state_v, state_ref, out_sem.at[6])
    state_out.start()
    energy_ref[...] = own[0:1] / own[1:2]
    scale = 1.0 / jnp.sqrt(f32(n))

    def outgoing(side):
        held_out, ref = ((lb_v, lb_ref), (rb_v, rb_ref))[side]
        return [
            pltpu.make_async_copy(
                held_out.at[pl.ds(start, rows)], ref.at[pl.ds(start, rows)],
                out_sem.at[3 * side + i],
            )
            for i, (start, rows, _) in enumerate(chunks)
        ]

    def extend_side(side, late):
        _, ops, out, _, arrival = sides[side]
        arrival.wait_recv()
        k = far_kept[side] * norm(totals(2 * side))
        first, second = (k.T, k) if side else (k, k.T)
        weight, streams = stationary(first), streamed(second)
        for i, (start, rows, _) in enumerate(chunks):
            if late and i > 0:
                prepare_chunk(side, i)
            extend(ops, weight, streams, out, scale, start, rows // n, n)
            outgoing(side)[i].start()

    def clear(side):
        out = (lb_v, rb_v)[side]
        out[...] = jnp.zeros_like(out)
        for copy in outgoing(side):
            copy.start()

    pl.when(s == 0)(lambda: clear(0))
    pl.when(s == nseg - 1)(lambda: clear(1))
    pl.when(jnp.logical_and(even, has_up))(lambda: extend_side(1, False))
    pl.when(jnp.logical_and(odd, has_down))(lambda: extend_side(0, False))
    pl.when(jnp.logical_and(even, has_down))(lambda: extend_side(0, True))
    pl.when(jnp.logical_and(odd, has_up))(lambda: extend_side(1, True))

    @pl.when(has_next)
    def _():
        for k in range(ITERS):
            send_v(k).wait_send()

    @pl.when(has_previous)
    def _():
        for k in range(ITERS):
            send_c(k).wait_send()

    send_environments(lambda copy: copy.wait_send())
    on_relay(lambda *way: pl.when(s == way[1])(lambda: from_relay(*way).wait_send()))
    pl.when(has_up)(lambda: kept_up.wait_send())
    pl.when(has_down)(lambda: kept_down.wait_send())
    per_segment(lambda step: per_peer(step, lambda peer, j: sum_copy(step, peer, j).wait_send()))
    for copy in outgoing(0) + outgoing(1) + [state_out]:
        copy.wait()


def write_out(*refs):
    loaded, sems = refs[8:12], refs[12]
    copies = []
    for i in range(4):
        rows = refs[i].shape[0]
        step = max(rows // 3, 128)
        for at in range(0, rows, step):
            size = min(step, rows - at)
            j = len(copies)
            part = (lambda ref: ref) if size == rows else (lambda ref: ref.at[pl.ds(at, size)])
            source, middle, target = part(refs[i]), part(loaded[i]), part(refs[4 + i])
            copies.append(
                (
                    pltpu.make_async_copy(source, middle, sems.at[0, j]),
                    pltpu.make_async_copy(middle, target, sems.at[1, j]),
                )
            )
    for load, _ in copies:
        load.start()
    for load, store in copies:
        load.wait()
        store.start()
    for _, store in copies:
        store.wait()


def shards(nseg, nblk, two_site, diag_left, diag_right, hop_left, hop_right, sector_sizes, ranks):
    n = two_site.shape[2]
    ndiag, nhop = diag_left.shape[2], hop_left.shape[2]
    nch = ndiag + nhop
    smem = pl.BlockSpec(memory_space=pltpu.SMEM)
    vmem = pl.BlockSpec(memory_space=pltpu.VMEM)
    hbm = pl.BlockSpec(memory_space=pltpu.HBM)
    dma = pltpu.SemaphoreType.DMA
    state, left, right, energy = pl.pallas_call(
        functools.partial(kernel, nseg, nblk, ndiag, nhop, n),
        out_shape=(
            jax.ShapeDtypeStruct((n, n), f32),
            jax.ShapeDtypeStruct((nch * n, n), f32),
            jax.ShapeDtypeStruct((nch * n, n), f32),
            jax.ShapeDtypeStruct((1, 1), f32),
        ),
        in_specs=[smem, smem] + [hbm] * 5,
        out_specs=(hbm, hbm, hbm, vmem),
        scratch_shapes=[
            pltpu.VMEM((nch * n, n), f32),
            pltpu.VMEM((nch * n, n), f32),
            pltpu.VMEM((nch * n, n), f32),
            pltpu.VMEM((nch * n, n), f32),
            pltpu.VMEM((n, n), f32),
            pltpu.VMEM((nch * n, n), f32),
            pltpu.VMEM((nch * n, n), f32),
            pltpu.VMEM((nch * n, 2 * n), bf16),
            pltpu.VMEM((nhop * n, 2 * n), bf16),
            pltpu.VMEM((nhop * n, 2 * n), bf16),
            pltpu.VMEM((nch * n, 2 * n), bf16),
            pltpu.VMEM((nch * n, 2 * n), bf16),
            pltpu.VMEM((nch * n, 2 * n), bf16),
            pltpu.VMEM((2 * n, nch * n), bf16),
            pltpu.VMEM((ITERS + 1, n, n), f32),
            pltpu.VMEM((ITERS + 1, n, n), f32),
            pltpu.VMEM((ITERS, n, n), f32),
            pltpu.VMEM((ITERS, n, n), f32),
            pltpu.VMEM((n, n), f32),
            pltpu.VMEM((2, n, n), f32),
            pltpu.VMEM((3, nblk, 8, n), f32),
            dma((5,)),
            dma((ITERS,)),
            dma((ITERS,)),
            dma((ITERS,)),
            dma((ITERS,)),
            dma((6,)),
            dma((6,)),
            dma((2,)),
            dma((2,)),
            dma((3, nblk)),
            dma((3, nblk)),
            dma((7,)),
            pltpu.VMEM((nhop * n - (nhop // 2 - 1) * n, n), f32),
            dma((2,)),
            dma((1,)),
        ],
        compiler_params=pltpu.CompilerParams(
            collective_id=0, has_side_effects=True, vmem_limit_bytes=57 * 1024 * 1024
        ),
        name="solve",
    )(
        sector_sizes, ranks,
        two_site.reshape(n, n),
        diag_left.reshape(ndiag * n, n),
        diag_right.reshape(ndiag * n, n),
        hop_left.reshape(nhop * n, n),
        hop_right.reshape(nhop * n, n),
    )
    left, right, state, energy = pl.pallas_call(
        write_out,
        out_shape=tuple(jax.ShapeDtypeStruct(x.shape, f32) for x in (left, right, state, energy)),
        in_specs=[hbm] * 4,
        out_specs=(hbm,) * 4,
        scratch_shapes=[pltpu.VMEM(x.shape, f32) for x in (left, right, state, energy)]
        + [dma((2, 8))],
        compiler_params=pltpu.CompilerParams(vmem_limit_bytes=57 * 1024 * 1024),
        name="write_out",
    )(left, right, state, energy)
    return (
        state.reshape(1, 1, n, n),
        left.reshape(1, 1, nch, n, n),
        right.reshape(1, 1, nch, n, n),
        energy.reshape(1),
    )


def solution(mesh):
    nseg, nblk = mesh.shape["seg"], mesh.shape["blk"]
    return jax.shard_map(
        functools.partial(shards, nseg, nblk),
        mesh=mesh,
        in_specs=(
            P("seg", "blk", None, None),
            P("seg", "blk", None, None, None),
            P("seg", "blk", None, None, None),
            P("seg", "blk", None, None, None),
            P("seg", "blk", None, None, None),
            P("seg", "blk"),
            P("seg", "blk"),
        ),
        out_specs=(
            P("seg", "blk", None, None),
            P("seg", "blk", None, None, None),
            P("seg", "blk", None, None, None),
            P("seg"),
        ),
        check_vma=False,
    )
```

```python
import functools

import jax
import jax.numpy as jnp
from jax import lax
from jax.experimental import pallas as pl
from jax.experimental.pallas import tpu as pltpu
from jax.sharding import PartitionSpec as P

ITERS = 4
BATCH = 4
MESH = pl.DeviceIdType.MESH
f32 = jnp.float32
bf16 = jnp.bfloat16
spectral_shift = 20.0


def split(x):
    hi = x.astype(bf16)
    lo = (x - hi.astype(f32)).astype(bf16)
    return hi, lo


def stationary(x):
    hi, lo = split(x)
    top = jnp.concatenate([hi, lo], 1)
    low = jnp.concatenate([hi, jnp.zeros_like(hi)], 1)
    return jnp.concatenate([top, low], 0)


def streamed(x):
    hi, lo = split(x)
    top = jnp.concatenate([hi, hi], 1)
    low = jnp.concatenate([lo, jnp.zeros_like(lo)], 1)
    return jnp.concatenate([top, low], 0)


def dot(a, b):
    return jnp.dot(a, b, preferred_element_type=f32)


def prepare(source, rows, target, at, transpose, n):
    x = source[pl.ds(rows, n), :]
    hi, lo = split(x.T if transpose else x)
    target[pl.ds(at, n), 0:n] = hi
    target[pl.ds(at, n), n : 2 * n] = lo


def first_stage(ops, start, count, weight, held, column, n):
    got = dot(ops[start : start + count * n, :], weight)
    got = got[:, 0:n] + got[:, n : 2 * n]
    hi, lo = split(got)
    for c in range(count):
        lanes = column + c * n
        held[0:n, lanes : lanes + n] = hi[c * n : (c + 1) * n]
        held[n : 2 * n, lanes : lanes + n] = lo[c * n : (c + 1) * n]


def second_stage(held, column, count, ops, start, n):
    got = dot(held[:, column : column + count * n], ops[start : start + count * n, :])
    return (got[0:n, 0:n] + got[0:n, n : 2 * n]) + (got[n : 2 * n, 0:n] + got[n : 2 * n, n : 2 * n])


def both_stages(left, right, start, count, weight, held, n):
    total, waiting = None, None
    for c in list(range(0, count, BATCH)) + [None]:
        if c is not None:
            size = min(BATCH, count - c)
            first_stage(left, start + c * n, size, weight, held, start + c * n, n)
        if waiting is not None:
            at, some = waiting
            term = second_stage(held, at, some, right, at, n)
            total = term if total is None else total + term
        waiting = None if c is None else (start + c * n, size)
    return total


def extend(ops, weight, rows, out, scale, start, count, n):
    got = dot(ops[start : start + count * n, :], weight)
    got = got[:, 0:n] + got[:, n : 2 * n]
    hi, lo = split(got)
    tops = [hi[c * n : (c + 1) * n] for c in range(count)]
    lows = [lo[c * n : (c + 1) * n] for c in range(count)]
    wide = jnp.concatenate([jnp.concatenate(tops, 1), jnp.concatenate(lows, 1)], 0)
    done = dot(rows, wide)
    done = (done[0:n] + done[n:]) * scale
    for c in range(count):
        out[start + c * n : start + (c + 1) * n, :] = done[:, c * n : (c + 1) * n]


def kernel(
    nseg, nblk, ndiag, nhop, n,
    size_ref, rank_ref, two_ref, dl_ref, dr_ref, hl_ref, hr_ref,
    state_ref, lb_ref, rb_ref, energy_ref,
    xl, yr, far_x, far_y, state_v, lb_v, rb_v, a2, at2, b2, bt2, fx2, fy2, held,
    v_buf, c_buf, rv, rc, kept, far_kept, sums,
    load_sem, v_send, v_recv, c_send, c_recv, x_send, x_recv, k_send, k_recv, s_send, s_recv, out_sem, relay, r_send, r_recv,
):
    s = lax.axis_index("seg")
    q = lax.axis_index("blk")
    nch = ndiag + nhop
    small = ndiag * n

    loads = [
        pltpu.make_async_copy(src, dst, load_sem.at[i])
        for i, (src, dst) in enumerate(
            (
                (two_ref, c_buf.at[ITERS]),
                (hl_ref, xl.at[pl.ds(small, nhop * n)]),
                (hr_ref, yr.at[pl.ds(small, nhop * n)]),
                (dl_ref, xl.at[pl.ds(0, small)]),
                (dr_ref, yr.at[pl.ds(0, small)]),
            )
        )
    ]
    for load in loads:
        load.start()

    def per_segment(action):
        action(0)
        pl.when(s < nseg - 1)(lambda: action(1))
        pl.when(s > 0)(lambda: action(-1))

    def per_peer(step, action):
        def body(j, carry):
            action(lax.rem(q + j, nblk), j)
            return carry

        lax.fori_loop(1 if step == 0 else 0, nblk, body, 0, unroll=nblk <= 8)

    barrier = pltpu.get_barrier_semaphore()

    def greet(step):
        per_peer(
            step,
            lambda peer, j: pl.semaphore_signal(
                barrier, inc=1, device_id={"seg": s + step, "blk": peer}, device_id_type=MESH
            ),
        )

    per_segment(greet)

    below, above = nseg // 2 - 1, nseg // 2
    relays = ((below, nseg - 1, above), (above, 0, below))

    def on_relay(action):
        for origin, via, target in relays:
            action(origin, via, target)

    def greet_relay(origin, via, target):
        for first, second in ((origin, via), (via, origin), (via, target), (target, via)):
            @pl.when(s == first)
            def _(second=second):
                pl.semaphore_signal(
                    barrier, inc=1, device_id={"seg": second, "blk": q}, device_id_type=MESH
                )

    on_relay(greet_relay)

    @pl.when(q == 0)
    def _():
        rv[...] = jnp.zeros_like(rv)

    @pl.when(q == nblk - 1)
    def _():
        rc[...] = jnp.zeros_like(rc)

    size = size_ref[0, 0]
    count = jnp.minimum(rank_ref[0, 0], size)
    row_at = lax.broadcasted_iota(jnp.int32, (n, n), 0)
    col_at = lax.broadcasted_iota(jnp.int32, (n, n), 1)
    live = jnp.where(jnp.maximum(row_at, col_at) < size, 1.0, 0.0).astype(f32)
    col_live = jnp.where(col_at < count, 1.0, 0.0).astype(f32)

    loads[0].wait()
    v_buf[0] = live * c_buf[ITERS]

    groups = 1 + jnp.minimum(s, 1) + jnp.minimum(nseg - 1 - s, 1)
    others = 0
    for place in (0, below, above, nseg - 1):
        others = others + 2 * (1 - jnp.minimum(jnp.maximum(s - place, place - s), 1))
    pl.semaphore_wait(barrier, groups * nblk - 1 + others)

    def remote(src, dst, send, recv, where):
        return pltpu.make_async_remote_copy(
            src_ref=src, dst_ref=dst, send_sem=send, recv_sem=recv,
            device_id=where, device_id_type=MESH,
        )

    def send_v(k):
        return remote(v_buf.at[k], rv.at[k], v_send.at[k], v_recv.at[k], {"seg": s, "blk": q + 1})

    def send_c(k):
        return remote(c_buf.at[k], rc.at[k], c_send.at[k], c_recv.at[k], {"seg": s, "blk": q - 1})

    up, down = {"seg": s + 1, "blk": q}, {"seg": s - 1, "blk": q}
    half = (nhop // 2 - 2) * n
    chunks = [(small, half, 1), (small + half, nhop * n - half, 1), (0, small, 0)]

    def environment(refs, far, first, where):
        return [
            remote(
                refs[hop].at[pl.ds(start - small * hop, rows)],
                far.at[pl.ds(start, rows)],
                x_send.at[first + i], x_recv.at[first + i], where,
            )
            for i, (start, rows, hop) in enumerate(chunks)
        ]

    to_up = environment((dl_ref, hl_ref), far_x, 0, up)
    to_down = environment((dr_ref, hr_ref), far_y, 3, down)
    kept_up = remote(kept, far_kept.at[0], k_send.at[0], k_recv.at[0], up)
    kept_down = remote(kept, far_kept.at[1], k_send.at[1], k_recv.at[1], down)

    has_next, has_previous = q < nblk - 1, q > 0
    has_up, has_down = s < nseg - 1, s > 0

    pl.when(has_next)(lambda: send_v(0).start())

    def to_relay(origin, via, target):
        start, rows, _ = chunks[1]
        source = hl_ref if origin < target else hr_ref
        return remote(
            source.at[pl.ds(start - small, rows)], relay, r_send.at[0], r_recv.at[0],
            {"seg": via, "blk": q},
        )

    def from_relay(origin, via, target):
        start, rows, _ = chunks[1]
        far, i = (far_x, 1) if origin < target else (far_y, 4)
        return remote(
            relay, far.at[pl.ds(start, rows)], r_send.at[1], x_recv.at[i],
            {"seg": target, "blk": q},
        )

    def send_environments(action):
        on_relay(lambda *way: pl.when(s == way[0])(lambda: action(to_relay(*way))))
        for copies, some, middle in ((to_up, has_up, below), (to_down, has_down, above)):
            pl.when(some)(lambda: action(copies[0]))
            pl.when(jnp.logical_and(some, s != middle))(lambda: action(copies[1]))
            pl.when(some)(lambda: action(copies[2]))

    def pass_on(*way):
        @pl.when(s == way[1])
        def _():
            to_relay(*way).wait_recv()
            from_relay(*way).start()

    send_environments(lambda copy: copy.start())

    loads[1].wait()
    loads[2].wait()
    for h in range(nhop):
        at = small + h * n
        prepare(xl, at, at2, h * n, True, n)
        prepare(yr, at, b2, h * n, False, n)

    def carried(k):
        c_buf[k] = both_stages(at2, b2, 0, nhop, stationary(v_buf[k]), held, n)
        pl.when(has_previous)(lambda: send_c(k).start())

    def finish(k):
        own = both_stages(a2, bt2, 0, ndiag, stationary(v_buf[k]), held, n)
        pl.when(has_previous)(lambda: send_v(k).wait_recv())
        own = own + both_stages(a2, bt2, small, nhop, stationary(rv[k]), held, n)
        pl.when(has_next)(lambda: send_c(k).wait_recv())
        applied = live * (own + rc[k])
        vector = spectral_shift * v_buf[k] - applied
        v_buf[k + 1] = vector
        return applied, vector

    carried(0)
    loads[3].wait()
    loads[4].wait()
    for c in range(nch):
        prepare(xl, c * n, a2, c * n, False, n)
        prepare(yr, c * n, bt2, c * n, True, n)
    finish(0)
    pl.when(has_next)(lambda: send_v(1).start())

    sides = ((far_x, fx2, lb_v, to_up, kept_up), (far_y, fy2, rb_v, to_down, kept_down))
    even = lax.rem(s, 2) == 0
    odd = jnp.logical_not(even)

    def prepare_chunk(side, i):
        far, ops, _, copies, _ = sides[side]
        start, rows, _ = chunks[i]
        copies[i].wait_recv()
        for at in range(start, start + rows, n):
            prepare(far, at, ops, at, side == 1, n)

    def prepare_side(side):
        for i in range(len(chunks)):
            prepare_chunk(side, i)

    def middle(k, carry):
        carried(k)
        finish(k)
        pl.when(has_next)(lambda: send_v(k + 1).start())
        pl.when(k == 1)(lambda: on_relay(pass_on))
        return carry

    lax.fori_loop(1, ITERS - 1, middle, 0)
    carried(ITERS - 1)
    pl.when(jnp.logical_and(even, has_up))(lambda: prepare_side(1))
    pl.when(jnp.logical_and(odd, has_down))(lambda: prepare_side(0))
    applied, vector = finish(ITERS - 1)
    last = v_buf[ITERS - 1]
    kept[...] = vector * col_live
    pl.when(has_up)(lambda: kept_up.start())
    pl.when(has_down)(lambda: kept_down.start())

    def rowsum(x):
        return jnp.sum(x, 0, keepdims=True)

    row8 = lax.broadcasted_iota(jnp.int32, (8, n), 0)
    tile = jnp.where(row8 == 0, rowsum(last * applied), 0.0)
    tile = jnp.where(row8 == 1, rowsum(last * last), tile)
    tile = jnp.where(row8 == 2, rowsum(vector * vector), tile)
    tile = jnp.where(row8 == 3, size.astype(f32) * (1.0 / n), tile)
    sums[1, q] = tile

    def sum_copy(step, peer, j):
        group = 1 - step
        return remote(
            sums.at[1, q], sums.at[group, q], s_send.at[group, j], s_recv.at[group, q],
            {"seg": s + step, "blk": peer},
        )

    def sum_arrival(group, peer):
        return remote(
            sums.at[1, q], sums.at[group, peer], s_send.at[group, 0], s_recv.at[group, peer],
            {"seg": s, "blk": peer},
        )

    per_segment(lambda step: per_peer(step, lambda peer, j: sum_copy(step, peer, j).start()))

    def totals(group):
        step = 0 if group == 1 else 1
        per_peer(step, lambda peer, j: sum_arrival(group, peer).wait_recv())
        total = sums[group, 0]
        for j in range(1, nblk):
            total = total + sums[group, j]
        return jnp.sum(total, 1, keepdims=True)

    def norm(total):
        return jnp.sqrt(total[3:4] * n / total[2:3])

    own = totals(1)
    state_v[...] = vector * norm(own)
    state_out = pltpu.make_async_copy(state_v, state_ref, out_sem.at[6])
    state_out.start()
    energy_ref[...] = own[0:1] / own[1:2]
    scale = 1.0 / jnp.sqrt(f32(n))

    def outgoing(side):
        held_out, ref = ((lb_v, lb_ref), (rb_v, rb_ref))[side]
        return [
            pltpu.make_async_copy(
                held_out.at[pl.ds(start, rows)], ref.at[pl.ds(start, rows)],
                out_sem.at[3 * side + i],
            )
            for i, (start, rows, _) in enumerate(chunks)
        ]

    def extend_side(side, late):
        _, ops, out, _, arrival = sides[side]
        arrival.wait_recv()
        k = far_kept[side] * norm(totals(2 * side))
        first, second = (k.T, k) if side else (k, k.T)
        weight, streams = stationary(first), streamed(second)
        for i, (start, rows, _) in enumerate(chunks):
            if late:
                prepare_chunk(side, i)
            extend(ops, weight, streams, out, scale, start, rows // n, n)
            outgoing(side)[i].start()

    def clear(side):
        out = (lb_v, rb_v)[side]
        out[...] = jnp.zeros_like(out)
        for copy in outgoing(side):
            copy.start()

    pl.when(s == 0)(lambda: clear(0))
    pl.when(s == nseg - 1)(lambda: clear(1))
    pl.when(jnp.logical_and(even, has_up))(lambda: extend_side(1, False))
    pl.when(jnp.logical_and(odd, has_down))(lambda: extend_side(0, False))
    pl.when(jnp.logical_and(even, has_down))(lambda: extend_side(0, True))
    pl.when(jnp.logical_and(odd, has_up))(lambda: extend_side(1, True))

    @pl.when(has_next)
    def _():
        for k in range(ITERS):
            send_v(k).wait_send()

    @pl.when(has_previous)
    def _():
        for k in range(ITERS):
            send_c(k).wait_send()

    send_environments(lambda copy: copy.wait_send())
    on_relay(lambda *way: pl.when(s == way[1])(lambda: from_relay(*way).wait_send()))
    pl.when(has_up)(lambda: kept_up.wait_send())
    pl.when(has_down)(lambda: kept_down.wait_send())
    per_segment(lambda step: per_peer(step, lambda peer, j: sum_copy(step, peer, j).wait_send()))
    for copy in outgoing(0) + outgoing(1) + [state_out]:
        copy.wait()


def write_out(*refs):
    loaded, sems = refs[8:12], refs[12]
    copies = []
    for i in range(4):
        rows = refs[i].shape[0]
        step = max(rows // 3, 128)
        for at in range(0, rows, step):
            size = min(step, rows - at)
            j = len(copies)
            part = (lambda ref: ref) if size == rows else (lambda ref: ref.at[pl.ds(at, size)])
            source, middle, target = part(refs[i]), part(loaded[i]), part(refs[4 + i])
            copies.append(
                (
                    pltpu.make_async_copy(source, middle, sems.at[0, j]),
                    pltpu.make_async_copy(middle, target, sems.at[1, j]),
                )
            )
    for load, _ in copies:
        load.start()
    for load, store in copies:
        load.wait()
        store.start()
    for _, store in copies:
        store.wait()


def shards(nseg, nblk, two_site, diag_left, diag_right, hop_left, hop_right, sector_sizes, ranks):
    n = two_site.shape[2]
    ndiag, nhop = diag_left.shape[2], hop_left.shape[2]
    nch = ndiag + nhop
    smem = pl.BlockSpec(memory_space=pltpu.SMEM)
    vmem = pl.BlockSpec(memory_space=pltpu.VMEM)
    hbm = pl.BlockSpec(memory_space=pltpu.HBM)
    dma = pltpu.SemaphoreType.DMA
    state, left, right, energy = pl.pallas_call(
        functools.partial(kernel, nseg, nblk, ndiag, nhop, n),
        out_shape=(
            jax.ShapeDtypeStruct((n, n), f32),
            jax.ShapeDtypeStruct((nch * n, n), f32),
            jax.ShapeDtypeStruct((nch * n, n), f32),
            jax.ShapeDtypeStruct((1, 1), f32),
        ),
        in_specs=[smem, smem] + [hbm] * 5,
        out_specs=(hbm, hbm, hbm, vmem),
        scratch_shapes=[
            pltpu.VMEM((nch * n, n), f32),
            pltpu.VMEM((nch * n, n), f32),
            pltpu.VMEM((nch * n, n), f32),
            pltpu.VMEM((nch * n, n), f32),
            pltpu.VMEM((n, n), f32),
            pltpu.VMEM((nch * n, n), f32),
            pltpu.VMEM((nch * n, n), f32),
            pltpu.VMEM((nch * n, 2 * n), bf16),
            pltpu.VMEM((nhop * n, 2 * n), bf16),
            pltpu.VMEM((nhop * n, 2 * n), bf16),
            pltpu.VMEM((nch * n, 2 * n), bf16),
            pltpu.VMEM((nch * n, 2 * n), bf16),
            pltpu.VMEM((nch * n, 2 * n), bf16),
            pltpu.VMEM((2 * n, nch * n), bf16),
            pltpu.VMEM((ITERS + 1, n, n), f32),
            pltpu.VMEM((ITERS + 1, n, n), f32),
            pltpu.VMEM((ITERS, n, n), f32),
            pltpu.VMEM((ITERS, n, n), f32),
            pltpu.VMEM((n, n), f32),
            pltpu.VMEM((2, n, n), f32),
            pltpu.VMEM((3, nblk, 8, n), f32),
            dma((5,)),
            dma((ITERS,)),
            dma((ITERS,)),
            dma((ITERS,)),
            dma((ITERS,)),
            dma((6,)),
            dma((6,)),
            dma((2,)),
            dma((2,)),
            dma((3, nblk)),
            dma((3, nblk)),
            dma((7,)),
            pltpu.VMEM((nhop * n - (nhop // 2 - 2) * n, n), f32),
            dma((2,)),
            dma((1,)),
        ],
        compiler_params=pltpu.CompilerParams(
            collective_id=0, has_side_effects=True, vmem_limit_bytes=57 * 1024 * 1024
        ),
        name="solve",
    )(
        sector_sizes, ranks,
        two_site.reshape(n, n),
        diag_left.reshape(ndiag * n, n),
        diag_right.reshape(ndiag * n, n),
        hop_left.reshape(nhop * n, n),
        hop_right.reshape(nhop * n, n),
    )
    left, right, state, energy = pl.pallas_call(
        write_out,
        out_shape=tuple(jax.ShapeDtypeStruct(x.shape, f32) for x in (left, right, state, energy)),
        in_specs=[hbm] * 4,
        out_specs=(hbm,) * 4,
        scratch_shapes=[pltpu.VMEM(x.shape, f32) for x in (left, right, state, energy)]
        + [dma((2, 8))],
        compiler_params=pltpu.CompilerParams(vmem_limit_bytes=57 * 1024 * 1024),
        name="write_out",
    )(left, right, state, energy)
    return (
        state.reshape(1, 1, n, n),
        left.reshape(1, 1, nch, n, n),
        right.reshape(1, 1, nch, n, n),
        energy.reshape(1),
    )


def solution(mesh):
    nseg, nblk = mesh.shape["seg"], mesh.shape["blk"]
    return jax.shard_map(
        functools.partial(shards, nseg, nblk),
        mesh=mesh,
        in_specs=(
            P("seg", "blk", None, None),
            P("seg", "blk", None, None, None),
            P("seg", "blk", None, None, None),
            P("seg", "blk", None, None, None),
            P("seg", "blk", None, None, None),
            P("seg", "blk"),
            P("seg", "blk"),
        ),
        out_specs=(
            P("seg", "blk", None, None),
            P("seg", "blk", None, None, None),
            P("seg", "blk", None, None, None),
            P("seg"),
        ),
        check_vma=False,
    )
```
